32 devices in a mesh: member: 2 (over y), band: 16 (over z, x, core).
Axes of the slice: x: 2, y: 2, z: 4, core: 2. Of those that a mesh axis runs over, the one named last changes fastest.
Arguments:
- fields: bfloat16 [4, 8192, 1024], P('member', 'band'), may hold values from -17.5 to 17.5
- w_qkv: bfloat16 [1024, 3072], replicated, may hold values from -0.1875 to 0.1875
- w_out: bfloat16 [1024, 1024], replicated, may hold values from -0.1875 to 0.1875
- decoder_weight: bfloat16 [96, 1024], replicated, may hold values from -0.1875 to 0.1875
- window_reach: int32 [16], replicated, may hold values from 1 to 128
- truth: float32 [96, 8192], P(None, 'band'), may hold values from -6 to 6
- radii: int32 [3], replicated, may hold values from 1 to 16
Outputs:
- mean_score: float32 [], replicated
- decoder_grad: float32 [96, 1024], replicated
- hidden_grad: bfloat16 [4, 8192, 1024], P('member', 'band')
The draws below stay inside these ranges and needn't reach their ends.
All inputs are finite; a program needn't handle non-finite values.
Results may differ from the reference program's by a relative error of at most 0.012.
The reference program's roundings to bfloat16 on the way count: a program that leaves them out, or rounds other values in their place, can miss the bound.
Values may be sent and summed in bfloat16 or wider, within the bound.
No kernel may reach another device: no remote copies, remote signals or barrier semaphores. Data moves between devices by JAX's collectives and lax.ppermute only.
A program may use at most 192 MiB of HBM per device.

```python
import math
import jax
import jax.numpy as jnp
from jax import lax

D = 1024
HEADS = 16
CHANNELS = 96
TOK_DEV = 512
WIN = 128
SCALES = 3
RMAX = 16
MEMBERS = 4
TOKENS = 8192


def draw_fields(key, part):
    dims_all = (MEMBERS, TOKENS, D)
    key_base = jax.random.fold_in(key, 0)
    values = jnp.clip(jax.random.normal(key_base, dims_all, jnp.float32), -6.0, 6.0)
    return values.astype(jnp.bfloat16)


def with_ends(drawn, key, low, high):
    extent = drawn.shape
    place = [jax.random.randint(jax.random.fold_in(key, axis), (), 0, extent[axis]) for axis in range(len(extent))]
    drawn = drawn.at[tuple(place)].set(low)
    longest = extent.index(max(extent))
    place[longest] = (place[longest] + 1) % extent[longest]
    return drawn.at[tuple(place)].set(high)


def shard_levels(rng, shape, shards, least, largest):
    gain = 1.0
    for dim, shards_of in shards:
        draws = jax.random.uniform(jax.random.fold_in(jax.random.fold_in(rng, 6), dim), (shards_of,), jnp.float32, least / len(shards), largest / len(shards))
        gain = gain * jnp.repeat(jnp.exp(draws), shape[dim] // shards_of).reshape((-1,) + (1,) * (len(shape) - 1 - dim))
    return gain


def gaussian(stream_key, shape, scale, reach, pieces=(), held_as=jnp.bfloat16):
    factor_of = shard_levels(stream_key, shape, pieces, -0.22, 0.18) if pieces else 1.0
    drawn = jax.random.normal(stream_key, shape, jnp.float32) * scale * factor_of
    return jnp.minimum(jnp.maximum(drawn, -reach), reach).astype(held_as)


def setup_inputs(seed: int = 0) -> dict:
    keys = jax.random.split(jax.random.key(seed), 8)
    fields = draw_fields(jax.random.fold_in(keys[7], 71), 0)
    w_qkv = gaussian(keys[1], (D, 3 * D), D ** -0.5, 0.1875)
    w_out = gaussian(keys[2], (D, D), D ** -0.5, 0.1875)
    decoder_weight = gaussian(keys[3], (CHANNELS, D), D ** -0.5, 0.1875)
    window_reach = with_ends(jax.random.randint(keys[4], (HEADS,), 1, WIN + 1), jax.random.fold_in(keys[4], 1), 1, WIN).astype(jnp.int32)
    truth = gaussian(keys[5], (CHANNELS, TOKENS), 1.0, 6.0, ((1, 16),), jnp.float32)
    radii = jax.random.randint(keys[6], (SCALES,), 1, RMAX + 1).astype(jnp.int32)
    return dict(fields=fields, w_qkv=w_qkv, w_out=w_out, decoder_weight=decoder_weight, window_reach=window_reach, truth=truth, radii=radii)


softness = 0.1

def kernel_table(radii):
    offsets = jnp.arange(-RMAX, RMAX + 1).astype(jnp.float32)
    reaches = radii.astype(jnp.float32)[:, None]
    spread_width = 0.5 * reaches
    weights_raw = jnp.exp(-(offsets[None, :] * offsets[None, :]) / (2.0 * spread_width * spread_width))
    weights_raw = jnp.where(jnp.abs(offsets)[None, :] <= reaches, weights_raw, 0.0)
    return weights_raw / lax.optimization_barrier(jnp.sum(weights_raw, axis=1, keepdims=True))

def filter_rows(padded, kernel, sequence_length):
    shaped = (kernel.shape[0],) + (1,) * (padded.ndim - 1)
    result = jnp.zeros((kernel.shape[0],) + padded.shape[1:-1] + (sequence_length,), jnp.float32)
    for position in range(kernel.shape[1]):
        result = result + kernel[:, position].reshape(shaped) * padded[..., position:position + sequence_length]
    return result

def soft_abs(values):
    return jnp.sqrt(values * values + softness * softness)

def fair_score(ensemble, observed):
    members_total = ensemble.shape[1]
    skill_term = jnp.zeros(observed.shape, jnp.float32)
    spread_term = jnp.zeros(observed.shape, jnp.float32)
    slopes = []
    for member_a in range(members_total):
        difference = ensemble[:, member_a] - observed
        magnitude = soft_abs(difference)
        skill_term = skill_term + magnitude
        slopes.append(difference / magnitude / members_total)
    pair_weight = 1.0 / (members_total * (members_total - 1))
    for member_a in range(members_total):
        for member_b in range(member_a + 1, members_total):
            difference = ensemble[:, member_a] - ensemble[:, member_b]
            magnitude = soft_abs(difference)
            spread_term = spread_term + magnitude
            slopes[member_a] = slopes[member_a] - pair_weight * difference / magnitude
            slopes[member_b] = slopes[member_b] + pair_weight * difference / magnitude
    scores = skill_term / members_total - pair_weight * spread_term
    return (scores, jnp.stack(slopes, axis=1))

def attend_member(member_fields, w_qkv, w_out, window_reach):
    tokens_total, width = member_fields.shape
    head_count = window_reach.shape[0]
    head_size = width // head_count
    packed = jnp.dot(member_fields, w_qkv, preferred_element_type=jnp.float32).astype(jnp.bfloat16)
    queries = packed[:, :width]
    key_pad = jnp.pad(packed[:, width:2 * width], ((WIN, WIN), (0, 0)))
    value_pad = jnp.pad(packed[:, 2 * width:], ((WIN, WIN), (0, 0)))
    key_count = TOK_DEV + 2 * WIN

    def one_block(block):
        start = (block * TOK_DEV).astype(jnp.int32)
        block_q = lax.dynamic_slice_in_dim(queries, start, TOK_DEV, 0).reshape(TOK_DEV, head_count, head_size).astype(jnp.float32)
        block_k = lax.dynamic_slice_in_dim(key_pad, start, key_count, 0).reshape(key_count, head_count, head_size).astype(jnp.float32)
        block_v = lax.dynamic_slice_in_dim(value_pad, start, key_count, 0).reshape(key_count, head_count, head_size).astype(jnp.float32)
        logits = jnp.einsum('qhd,khd->hqk', block_q, block_k) * head_size ** (-0.5)
        query_pos = start + jnp.arange(TOK_DEV, dtype=jnp.int32)
        key_pos = start - WIN + jnp.arange(key_count, dtype=jnp.int32)
        offset = key_pos[None, :] - query_pos[:, None]
        inside = (key_pos >= 0) & (key_pos < tokens_total)
        allowed = (jnp.abs(offset)[None] <= window_reach[:, None, None]) & inside[None, None, :]
        logits = jnp.where(allowed, logits, -1e+30)
        peak = lax.optimization_barrier(jnp.max(logits, axis=2, keepdims=True))
        expo = jnp.exp(logits - peak)
        probs = (expo / lax.optimization_barrier(jnp.sum(expo, axis=2, keepdims=True))).astype(jnp.bfloat16)
        mixed = jnp.einsum('hqk,khd->qhd', probs.astype(jnp.float32), block_v).astype(jnp.bfloat16)
        return mixed.reshape(TOK_DEV, width)
    attended = lax.map(one_block, jnp.arange(tokens_total // TOK_DEV, dtype=jnp.int32)).reshape(tokens_total, width)
    mixed_out = jnp.dot(attended, w_out, preferred_element_type=jnp.float32) + member_fields.astype(jnp.float32)
    return mixed_out.astype(jnp.bfloat16)

def reference(fields, w_qkv, w_out, decoder_weight, window_reach, truth, radii):
    hidden_state = jnp.stack([attend_member(fields[member_index], w_qkv, w_out, window_reach) for member_index in range(MEMBERS)])
    predicted_fields = jnp.einsum('ly,pey->ple', decoder_weight.astype(jnp.float32), hidden_state.astype(jnp.float32))
    kernel = kernel_table(radii)
    sequence_length = predicted_fields.shape[2]
    stacked_scales = jnp.concatenate([predicted_fields, truth.astype(jnp.float32)[None]], axis=0)
    padded = jnp.pad(stacked_scales, ((0, 0), (0, 0), (RMAX, RMAX)))
    smoothed = filter_rows(padded[None], kernel, sequence_length)
    scores, slopes = fair_score(smoothed[:, :MEMBERS], smoothed[:, MEMBERS])
    adjoint = filter_rows(jnp.pad(slopes, ((0, 0), (0, 0), (0, 0), (RMAX, RMAX))), kernel, sequence_length)
    cotangent = lax.optimization_barrier(jnp.sum(adjoint, axis=0)).astype(jnp.bfloat16)
    hidden_grad = jnp.einsum('mct,cd->mtd', cotangent.astype(jnp.float32), decoder_weight.astype(jnp.float32)).astype(jnp.bfloat16)
    decoder_grad = jnp.einsum('mct,mtd->cd', cotangent.astype(jnp.float32), hidden_state.astype(jnp.float32)) / math.sqrt(MEMBERS * sequence_length)
    mean_score = jnp.sum(scores) / (SCALES * CHANNELS * sequence_length)
    return (mean_score, decoder_grad, hidden_grad)
```

```python
import functools
import math

import jax
import jax.numpy as jnp
from jax import lax
from jax.experimental import pallas as pl
from jax.experimental.pallas import tpu as pltpu
from jax.sharding import PartitionSpec as P

WIN = 128
RMAX = 16
MARGIN = 2 * RMAX
HALO = WIN + MARGIN
LANES = 128
KEYS = 3 * LANES
EDGE = HALO
SUB = EDGE // 2
FRAME = EDGE + 2 * WIN
SCORE_ROWS = 144
SOFT = 0.1 * 0.1
F32 = jnp.float32
BF16 = jnp.bfloat16
NEG = -1e30
NT = (((1,), (1,)), ((), ()))
TN = (((0,), (0,)), ((), ()))


def mm(a, b):
    return jnp.dot(a, b, preferred_element_type=F32)


def half_masks():
    lane = lax.broadcasted_iota(jnp.int32, (1, LANES), 1)
    low = jnp.where(lane < LANES // 2, 1.0, 0.0).astype(BF16)
    return low, (1.0 - low.astype(F32)).astype(BF16)


def put_keys(kz, m, p, rows, piece):
    for h, mask in enumerate(half_masks()):
        kz[m, p, h, rows, :] = piece * mask


def put_values(vz, m, p, rows, piece):
    for h, mask in enumerate(half_masks()):
        vz[m, p, h, rows, :LANES] = piece * mask


def put_ones(vz, pairs):
    shape = vz.shape[:2] + vz.shape[3:4] + (LANES,)
    for h, mask in enumerate(half_masks()):
        vz[:, :, h, :, LANES:] = jnp.broadcast_to(mask.reshape(1, 1, 1, LANES), shape)


def attend(q, kz, vz, m, p, start, offset, reach, valid):
    rows = q.shape[0]
    window = pl.ds(start, KEYS)
    keys = jnp.concatenate([kz[m, p, 0, window, :], kz[m, p, 1, window, :]], axis=0)
    values = jnp.concatenate([vz[m, p, 0, window, :], vz[m, p, 1, window, :]], axis=0)
    logits = lax.dot_general(q, keys, NT, preferred_element_type=F32)
    qpos = lax.broadcasted_iota(jnp.int32, (rows, KEYS), 0) + offset
    kpos = lax.broadcasted_iota(jnp.int32, (rows, KEYS), 1)
    away = jnp.abs(qpos - kpos)
    if valid is not None:
        low, high = valid
        away = jnp.where((kpos >= low) & (kpos < high), away, 1 << 20)
    parts = []
    for h in range(2):
        one = jnp.where(away <= reach[h], logits[:, h * KEYS : (h + 1) * KEYS], NEG)
        peak = jnp.max(one, axis=1, keepdims=True)
        parts.append(jnp.exp(one - peak).astype(BF16))
    mixed = mm(jnp.concatenate(parts, axis=1), values)
    return (mixed[:, :LANES] / mixed[:, LANES:]).astype(BF16)


def main_kernel(scale, info, x, xh, wq, wk, wv, wo, dec, q_out, k_out, v_out, hid, fc, kz, vz, qs, att, res):
    step = pl.program_id(0)
    members, own, width = x.shape
    cols = wq.shape[1]
    pairs = cols // LANES
    core = info[0]
    lower = core == 1
    halo_at = jnp.where(lower, 0, HALO + own)
    near = jnp.where(lower, WIN, 0)
    edge = jnp.where(lower, 0, own - WIN + MARGIN)

    @pl.when(step == 0)
    def _():
        put_ones(vz, pairs)

    flat = x[...].reshape(members * own, width)
    flat_halo = xh[...].reshape(members * HALO, width)
    k_own = mm(flat, wk[...]).astype(BF16)
    k_halo = mm(flat_halo, wk[...]).astype(BF16)
    v_own = mm(flat, wv[...]).astype(BF16)
    v_halo = mm(flat_halo, wv[...]).astype(BF16)
    q_own = mm(flat, wq[...]).astype(BF16)
    near_rows = jnp.concatenate(
        [xh[m, pl.ds(pl.multiple_of(near, 32), MARGIN), :] for m in range(members)], axis=0
    )
    q_halo = mm(near_rows, wq[...]).astype(BF16)
    k_out[...] = k_own.reshape(members, own, cols)
    v_out[...] = v_own.reshape(members, own, cols)
    q_own = (q_own.astype(F32) * scale).astype(BF16)
    q_halo = (q_halo.astype(F32) * scale).astype(BF16)
    q_out[...] = q_own.reshape(members, own, cols)
    own_rows = pl.ds(HALO, own)
    halo_rows = pl.ds(pl.multiple_of(halo_at, 32), HALO)
    q_at = pl.ds(pl.multiple_of(halo_at + near, 32), MARGIN)
    for m in range(members):
        qs[m, own_rows, :] = q_own[m * own : (m + 1) * own]
        qs[m, q_at, :] = q_halo[m * MARGIN : (m + 1) * MARGIN]
        for p in range(pairs):
            lanes = slice(p * LANES, (p + 1) * LANES)
            put_keys(kz, m, p, own_rows, k_own[m * own : (m + 1) * own, lanes])
            put_keys(kz, m, p, halo_rows, k_halo[m * HALO : (m + 1) * HALO, lanes])
            put_values(vz, m, p, own_rows, v_own[m * own : (m + 1) * own, lanes])
            put_values(vz, m, p, halo_rows, v_halo[m * HALO : (m + 1) * HALO, lanes])

    inner = own - 2 * WIN
    for p in range(pairs):
        reach = [info[4 + (step * pairs + p) * 2 + h] for h in range(2)]
        lanes = slice(p * LANES, (p + 1) * LANES)
        out_lanes = pl.ds(pl.multiple_of(step * cols + p * LANES, LANES), LANES)
        for m in range(members):
            for b in range(inner // WIN):
                first = HALO + WIN + b * WIN
                q = qs[m, first : first + WIN, lanes]
                att[m, b * WIN : (b + 1) * WIN, out_lanes] = attend(
                    q, kz, vz, m, p, first - WIN, WIN, reach, None
                )
            for b in range(2):
                q_rows = pl.ds(pl.multiple_of(edge + WIN + b * SUB, 16), SUB)
                q = qs[m, q_rows, lanes]
                start = pl.multiple_of(edge + b * (FRAME - KEYS), 32)
                att[m, inner + b * SUB : inner + (b + 1) * SUB, out_lanes] = attend(
                    q, kz, vz, m, p, start, WIN + b * (SUB + KEYS - FRAME), reach, None
                )

    @pl.when(step == pl.num_programs(0) - 1)
    def _():
        own_first = jnp.where(lower, MARGIN, 0)
        from_own = pl.ds(pl.multiple_of(jnp.where(lower, 0, own - WIN), 32), WIN)
        for m in range(members):
            res[pl.ds(pl.multiple_of(own_first, 32), WIN), :] = x[m, from_own, :]
            res[pl.ds(pl.multiple_of(jnp.where(lower, 0, WIN), 32), MARGIN), :] = xh[
                m, pl.ds(pl.multiple_of(near, 32), MARGIN), :
            ]
            mixed = mm(att[m], wo[...])
            hid[m, :inner, :] = (mixed[:inner] + x[m, WIN : own - WIN, :].astype(F32)).astype(BF16)
            hid[m, inner:, :] = (mixed[inner:] + res[...].astype(F32)).astype(BF16)
            fc[m] = lax.dot_general(hid[m], dec[...], NT, preferred_element_type=F32)


def edge_kernel(scale, info, x, xh, wq, wk, wv, qi, ki, vi, wo, dec, hid, fc, kz, vz, qs, att, res):
    step = pl.program_id(0)
    members, own, width = x.shape
    cols = wq.shape[1]
    pairs = cols // LANES
    lower = info[0] == 0
    halo_at = jnp.where(lower, 0, 2 * WIN)
    own_at = jnp.where(lower, HALO, 0)
    near = jnp.where(lower, WIN, 0)
    low = jnp.where(info[1] == 1, HALO, 0)
    high = jnp.where(info[2] == 1, 2 * WIN, FRAME)

    @pl.when(step == 0)
    def _():
        put_ones(vz, pairs)

    flat_halo = xh[...].reshape(members * HALO, width)
    k_halo = mm(flat_halo, wk[...]).astype(BF16)
    v_halo = mm(flat_halo, wv[...]).astype(BF16)
    near_rows = jnp.concatenate(
        [xh[m, pl.ds(pl.multiple_of(near, 32), MARGIN), :] for m in range(members)], axis=0
    )
    q_halo = mm(near_rows, wq[...]).astype(BF16)
    q_halo = (q_halo.astype(F32) * scale).astype(BF16)
    own_rows = pl.ds(pl.multiple_of(own_at, 32), 2 * WIN)
    halo_rows = pl.ds(pl.multiple_of(halo_at, 32), HALO)
    for m in range(members):
        qs[m, pl.ds(pl.multiple_of(jnp.where(lower, MARGIN, 0), 32), WIN), :] = qi[m]
        qs[m, pl.ds(pl.multiple_of(jnp.where(lower, 0, WIN), 32), MARGIN), :] = q_halo[
            m * MARGIN : (m + 1) * MARGIN
        ]
        for p in range(pairs):
            lanes = slice(p * LANES, (p + 1) * LANES)
            put_keys(kz, m, p, own_rows, ki[m, :, lanes])
            put_keys(kz, m, p, halo_rows, k_halo[m * HALO : (m + 1) * HALO, lanes])
            put_values(vz, m, p, own_rows, vi[m, :, lanes])
            put_values(vz, m, p, halo_rows, v_halo[m * HALO : (m + 1) * HALO, lanes])

    for p in range(pairs):
        reach = [info[4 + (step * pairs + p) * 2 + h] for h in range(2)]
        lanes = slice(p * LANES, (p + 1) * LANES)
        out_lanes = pl.ds(pl.multiple_of(step * cols + p * LANES, LANES), LANES)
        for m in range(members):
            for b in range(2):
                start = b * (FRAME - KEYS)
                att[m, b * SUB : (b + 1) * SUB, out_lanes] = attend(
                    qs[m, b * SUB : (b + 1) * SUB, lanes],
                    kz,
                    vz,
                    m,
                    p,
                    start,
                    WIN + b * SUB - start,
                    reach,
                    (low - start, high - start),
                )

    @pl.when(step == pl.num_programs(0) - 1)
    def _():
        from_own = pl.ds(pl.multiple_of(jnp.where(lower, 0, own - WIN), 32), WIN)
        for m in range(members):
            res[m, pl.ds(pl.multiple_of(jnp.where(lower, MARGIN, 0), 32), WIN), :] = x[m, from_own, :]
            res[m, pl.ds(pl.multiple_of(jnp.where(lower, 0, WIN), 32), MARGIN), :] = xh[
                m, pl.ds(pl.multiple_of(near, 32), MARGIN), :
            ]
        mixed = mm(att[...].reshape(members * EDGE, width), wo[...])
        hidden = (mixed + res[...].reshape(members * EDGE, width).astype(F32)).astype(BF16)
        hid[...] = hidden.reshape(members, EDGE, width)
        fc[...] = lax.dot_general(hidden, dec[...], NT, preferred_element_type=F32).reshape(
            members, EDGE, dec.shape[0]
        )


def toeplitz(radii, scale_index, rows, cols):
    reach = radii[scale_index].astype(F32)
    spread = 0.5 * reach
    twice = 2.0 * spread * spread

    def weigh(shape, shift):
        away = lax.broadcasted_iota(jnp.int32, shape, 1) - shift
        far = jnp.abs(away).astype(F32)
        return jnp.where(far <= reach, jnp.exp(-(far * far) / twice), 0.0)

    line = weigh((8, LANES), RMAX)
    total = jnp.sum(line, axis=1, keepdims=True)[:1]
    shift = lax.broadcasted_iota(jnp.int32, (rows, cols), 0) + RMAX
    return weigh((rows, cols), shift) / total


def split(values):
    high = values.astype(BF16)
    return high, (values - high.astype(F32)).astype(BF16)


def score_kernel(
    channels, members_total, info, radii, fa, fb, ga, gb, truth, t_near, t_far, hid_a, hid_b, cot, part, fh, fl, sh, sl
):
    members, _, _ = fa.shape
    own = truth.shape[0]
    scales = radii.shape[0]
    inner = own - 2 * WIN
    rows = SCORE_ROWS
    window = 2 * LANES
    lower = info[0] == 0
    begins, ends = info[1] == 1, info[2] == 1
    far_at = pl.ds(pl.multiple_of(jnp.where(lower, 0, inner + EDGE), 32), EDGE)
    near_at = pl.ds(pl.multiple_of(jnp.where(lower, inner + EDGE, 0), 32), EDGE)
    total_rows = own + 2 * MARGIN

    def put(at, column, values):
        lanes = slice(column * LANES, (column + 1) * LANES)
        fh[at, lanes], fl[at, lanes] = split(values)

    for side, (f_main, f_far) in enumerate(((fa, fb), (ga, gb))):
        for m in range(members):
            column = side * members + m
            put(pl.ds(EDGE, inner), column, f_main[m, :inner, :])
            put(near_at, column, f_main[m, inner:, :])
            put(far_at, column, f_far[m])
    put(pl.ds(MARGIN, own), 2 * members, truth[...])
    put(pl.ds(pl.multiple_of(jnp.where(lower, 0, MARGIN + own), 32), MARGIN), 2 * members, t_far[...])
    put(pl.ds(pl.multiple_of(jnp.where(lower, MARGIN + own, 0), 32), MARGIN), 2 * members, t_near[...])
    for ref in (fh, fl):
        ref[total_rows:, :] = jnp.zeros((ref.shape[0] - total_rows, ref.shape[1]), BF16)

        @pl.when(begins)
        def _():
            ref[:MARGIN, :] = jnp.zeros((MARGIN, ref.shape[1]), BF16)

        @pl.when(ends)
        def _():
            ref[MARGIN + own : total_rows, :] = jnp.zeros((MARGIN, ref.shape[1]), BF16)

    tiles = -(-(own + 2 * RMAX) // rows)
    for ref in (sh, sl):
        spare = ref.shape[1] - tiles * rows
        ref[:, tiles * rows :, :] = jnp.zeros((scales, spare, ref.shape[2]), BF16)

    weights = [split(toeplitz(radii, s, rows, window)) for s in range(scales)]
    forward = jnp.concatenate([jnp.concatenate([h, h, l], axis=1) for h, l in weights], axis=0)
    backward = jnp.concatenate(
        [h[:LANES] for h, l in weights] + [h[:LANES] for h, l in weights] + [l[:LANES] for h, l in weights],
        axis=1,
    )
    first_valid = jnp.where(begins, RMAX, 0)
    last_valid = jnp.where(ends, RMAX + own, 2 * RMAX + own)
    pair_weight = 1.0 / (members_total * (members_total - 1))
    others = 2 * members
    total = jnp.zeros((rows, LANES), F32)
    for tile in range(tiles):
        at = pl.ds(tile * rows, window)
        stacked = jnp.concatenate([fh[at, :], fl[at, :], fh[at, :]], axis=0)
        smooth = mm(forward, stacked)
        line = lax.broadcasted_iota(jnp.int32, (rows, LANES), 0) + tile * rows
        valid = jnp.where((line >= first_valid) & (line < last_valid), 1.0, 0.0)
        tile_score = jnp.zeros((rows, LANES), F32)
        for s in range(scales):
            values = [
                smooth[s * rows : (s + 1) * rows, i * LANES : (i + 1) * LANES] for i in range(others + 1)
            ]

            def gap(a, b):
                away = values[a] - values[b]
                square = away * away + SOFT
                inverse = lax.rsqrt(square)
                return away * inverse, square * inverse

            skill = jnp.zeros((rows, LANES), F32)
            spread = jnp.zeros((rows, LANES), F32)
            slopes = []
            cross = [jnp.zeros((rows, LANES), F32) for _ in range(members)]
            for m in range(members):
                slope, size = gap(m, others)
                skill = skill + size
                slopes.append(slope)
            for a in range(members):
                for b in range(a + 1, others):
                    slope, size = gap(a, b)
                    cross[a] = cross[a] + slope
                    if b < members:
                        cross[b] = cross[b] - slope
                        spread = spread + size
                    else:
                        spread = spread + 0.5 * size
            tile_score = tile_score + (skill * (1.0 / members_total) - pair_weight * spread)
            for m in range(members):
                slope = (slopes[m] * (1.0 / members_total) - pair_weight * cross[m]) * valid
                keep, lanes = pl.ds(tile * rows, rows), slice(m * LANES, (m + 1) * LANES)
                sh[s, keep, lanes], sl[s, keep, lanes] = split(slope)
        mine = (line >= RMAX) & (line < RMAX + own)
        total = total + jnp.where(mine, tile_score, 0.0)
    lane = lax.broadcasted_iota(jnp.int32, (rows, LANES), 1)
    total = jnp.where(lane < channels, total, 0.0)
    score = jnp.sum(jnp.sum(total, axis=0, keepdims=True), axis=1, keepdims=True)

    for tile in range(own // LANES):
        at = pl.ds(tile * LANES, window)
        high = [sh[s, at, :] for s in range(scales)]
        low = [sl[s, at, :] for s in range(scales)]
        stacked = jnp.concatenate(high + low + high, axis=0)
        cot[tile * LANES : (tile + 1) * LANES, :] = mm(backward, stacked).astype(BF16)

    near_own = pl.ds(pl.multiple_of(jnp.where(lower, own - WIN, 0), 32), WIN)
    far_own = pl.ds(pl.multiple_of(jnp.where(lower, 0, own - WIN), 32), WIN)
    near_skip = pl.multiple_of(jnp.where(lower, 0, MARGIN), 32)
    far_skip = pl.multiple_of(jnp.where(lower, MARGIN, 0), 32)
    width = hid_a.shape[2]
    grad = jnp.zeros((LANES, width), F32)
    for m in range(members):
        lanes = slice(m * LANES, (m + 1) * LANES)
        for c_rows, ref, h_rows in (
            (pl.ds(WIN, inner), hid_a, pl.ds(0, inner)),
            (near_own, hid_a, pl.ds(inner + near_skip, WIN)),
            (far_own, hid_b, pl.ds(far_skip, WIN)),
        ):
            grad = grad + lax.dot_general(cot[c_rows, lanes], ref[m, h_rows, :], TN, preferred_element_type=F32)
    keep = part.shape[1]
    line = lax.broadcasted_iota(jnp.int32, (keep, LANES), 0)
    score_high = score.astype(BF16).astype(F32)
    extra = jnp.where(line == channels, score_high, score - score_high)
    for chunk in range(width // LANES):
        piece = grad[:keep, chunk * LANES : (chunk + 1) * LANES]
        part[chunk] = jnp.where(line < channels, piece, jnp.where(line < channels + 2, extra, 0.0)).astype(BF16)


def grad_kernel(cot, dec, out):
    out[0] = mm(cot[...], dec[...]).astype(BF16)


def swap_pairs(count, first):
    pairs = []
    for i in range(first, count - 1, 2):
        pairs += [(i, i + 1), (i + 1, i)]
    return pairs


def reduce_all(part, mesh_shape):
    bands, count = mesh_shape["band"], mesh_shape["member"]
    half = part.shape[0] // 2
    core = lax.axis_index("band") % 2

    def swap(values, axis, size, bit):
        return lax.ppermute(values, axis, [(i, i ^ bit) for i in range(size)])

    mine = lax.dynamic_slice_in_dim(part, core * half, half, 0)
    theirs = lax.dynamic_slice_in_dim(part, (1 - core) * half, half, 0)
    total = mine.astype(F32) + swap(theirs, "band", bands, 1).astype(F32)
    bit = 1
    while bit < count:
        total = total + swap(total.astype(BF16), "member", count, bit).astype(F32)
        bit *= 2
    bit = 2
    while bit < bands:
        total = total + swap(total.astype(BF16), "band", bands, bit).astype(F32)
        bit *= 2
    other = swap(total.astype(BF16), "band", bands, 1).astype(F32)
    first = jnp.where(core == 0, total, other)
    second = jnp.where(core == 0, other, total)
    return jnp.concatenate([first, second], axis=0)


def local(mesh_shape, fields, w_qkv, w_out, decoder_weight, window_reach, truth, radii):
    members, own, width = fields.shape
    heads = window_reach.shape[0]
    head = width // heads
    channels = decoder_weight.shape[0]
    scales = radii.shape[0]
    bands, member_count = mesh_shape["band"], mesh_shape["member"]
    members_total = members * member_count
    scale = head**-0.5
    band = lax.axis_index("band")
    core = band % 2
    info = jnp.concatenate(
        [
            jnp.stack([core, band == 0, band == bands - 1, 0]).astype(jnp.int32),
            window_reach.astype(jnp.int32),
        ]
    )
    inside, across = swap_pairs(bands, 0), swap_pairs(bands, 1)

    def exchange(block, dim, size):
        last = block.shape[dim] - size
        near = lax.dynamic_slice_in_dim(block, (1 - core) * last, size, dim)
        far = lax.dynamic_slice_in_dim(block, core * last, size, dim)
        return lax.ppermute(near, "band", inside), lax.ppermute(far, "band", across)

    x_near, x_far = exchange(fields, 1, HALO)
    truth_t = jnp.pad(truth.T, ((0, 0), (0, LANES - channels)))
    t_near, t_far = exchange(truth_t, 0, MARGIN)
    dec = jnp.pad(decoder_weight, ((0, LANES - channels), (0, 0)))

    cols = 2 * LANES
    steps = width // cols
    pairs = cols // LANES
    whole = lambda shape: pl.BlockSpec(shape, lambda i, s: (0,) * len(shape))
    weight = lambda third: pl.BlockSpec((width, cols), lambda i, s: (0, third * steps + i))
    inner = own - 2 * WIN
    main_rows = inner + EDGE
    col_block = lambda rows: pl.BlockSpec((members, rows, cols), lambda i, s: (0, 0, i))
    params = pltpu.CompilerParams(
        dimension_semantics=("arbitrary",), vmem_limit_bytes=48 * 1024 * 1024
    )
    q_own, k_own, v_own, hid_a, fc_a = pl.pallas_call(
        functools.partial(main_kernel, scale),
        grid_spec=pltpu.PrefetchScalarGridSpec(
            num_scalar_prefetch=1,
            grid=(steps,),
            in_specs=[
                whole((members, own, width)),
                whole((members, HALO, width)),
                weight(0),
                weight(1),
                weight(2),
                whole((width, width)),
                whole((LANES, width)),
            ],
            out_specs=[
                col_block(own),
                col_block(own),
                col_block(own),
                whole((members, main_rows, width)),
                whole((members, main_rows, LANES)),
            ],
            scratch_shapes=[
                pltpu.VMEM((members, pairs, 2, own + 2 * HALO, LANES), BF16),
                pltpu.VMEM((members, pairs, 2, own + 2 * HALO, 2 * LANES), BF16),
                pltpu.VMEM((members, own + 2 * HALO, cols), BF16),
                pltpu.VMEM((members, main_rows, width), BF16),
                pltpu.VMEM((EDGE, width), BF16),
            ],
        ),
        out_shape=[jax.ShapeDtypeStruct((members, own, width), BF16)] * 3
        + [
            jax.ShapeDtypeStruct((members, main_rows, width), BF16),
            jax.ShapeDtypeStruct((members, main_rows, LANES), F32),
        ],
        compiler_params=params,
        cost_estimate=pl.CostEstimate(
            flops=2 * members * own * width * 5 * width, bytes_accessed=24 << 20, transcendentals=1 << 22
        ),
    )(info, fields, x_near, w_qkv, w_qkv, w_qkv, w_out, dec)

    member_pairs = [(i, i ^ 1) for i in range(member_count)]
    other_a = lax.ppermute(fc_a, "member", member_pairs)

    far_block = lambda rows, last: pl.BlockSpec((members, rows, cols), lambda i, s: (0, s[0] * last, i))
    hid_b, fc_b = pl.pallas_call(
        functools.partial(edge_kernel, scale),
        grid_spec=pltpu.PrefetchScalarGridSpec(
            num_scalar_prefetch=1,
            grid=(steps,),
            in_specs=[
                whole((members, own, width)),
                whole((members, HALO, width)),
                weight(0),
                weight(1),
                weight(2),
                far_block(WIN, own // WIN - 1),
                far_block(2 * WIN, own // (2 * WIN) - 1),
                far_block(2 * WIN, own // (2 * WIN) - 1),
                whole((width, width)),
                whole((LANES, width)),
            ],
            out_specs=[whole((members, EDGE, width)), whole((members, EDGE, LANES))],
            scratch_shapes=[
                pltpu.VMEM((members, pairs, 2, FRAME, LANES), BF16),
                pltpu.VMEM((members, pairs, 2, FRAME, 2 * LANES), BF16),
                pltpu.VMEM((members, EDGE, cols), BF16),
                pltpu.VMEM((members, EDGE, width), BF16),
                pltpu.VMEM((members, EDGE, width), BF16),
            ],
        ),
        out_shape=[
            jax.ShapeDtypeStruct((members, EDGE, width), BF16),
            jax.ShapeDtypeStruct((members, EDGE, LANES), F32),
        ],
        compiler_params=params,
        cost_estimate=pl.CostEstimate(
            flops=2 * members * own * width * 2 * width, bytes_accessed=14 << 20, transcendentals=1 << 21
        ),
    )(info, fields, x_far, w_qkv, w_qkv, w_qkv, q_own, k_own, v_own, w_out, dec)
    other_b = lax.ppermute(fc_b, "member", member_pairs)

    keep = channels + 16
    chunks = width // LANES
    tiles = -(-(own + 2 * RMAX) // SCORE_ROWS)
    f_rows = (tiles - 1) * SCORE_ROWS + 2 * LANES
    s_rows = own + LANES
    smem = pl.BlockSpec(memory_space=pltpu.SMEM)
    vmem = pl.BlockSpec(memory_space=pltpu.VMEM)
    cot, part = pl.pallas_call(
        functools.partial(score_kernel, channels, members_total),
        in_specs=[smem, smem] + [vmem] * 9,
        out_specs=[vmem, vmem],
        out_shape=[
            jax.ShapeDtypeStruct((own, members * LANES), BF16),
            jax.ShapeDtypeStruct((chunks, keep, LANES), BF16),
        ],
        scratch_shapes=[
            pltpu.VMEM((f_rows, (2 * members + 1) * LANES), BF16),
            pltpu.VMEM((f_rows, (2 * members + 1) * LANES), BF16),
            pltpu.VMEM((scales, s_rows, members * LANES), BF16),
            pltpu.VMEM((scales, s_rows, members * LANES), BF16),
        ],
        compiler_params=pltpu.CompilerParams(vmem_limit_bytes=48 * 1024 * 1024),
    )(info, radii, fc_a, fc_b, other_a, other_b, truth_t, t_near, t_far, hid_a, hid_b)

    hidden_grad = pl.pallas_call(
        grad_kernel,
        grid=(members, 2),
        in_specs=[
            pl.BlockSpec((own // 2, LANES), lambda m, h: (h, m)),
            pl.BlockSpec((LANES, width), lambda m, h: (0, 0)),
        ],
        out_specs=pl.BlockSpec((1, own // 2, width), lambda m, h: (m, h, 0)),
        out_shape=jax.ShapeDtypeStruct((members, own, width), BF16),
        cost_estimate=pl.CostEstimate(
            flops=2 * members * own * LANES * width, bytes_accessed=3 << 20, transcendentals=0
        ),
    )(cot, dec)

    summed = reduce_all(part, mesh_shape)
    decoder_grad = summed[:, :channels, :].transpose(1, 0, 2).reshape(channels, width)
    decoder_grad = decoder_grad / math.sqrt(members_total * own * bands)
    mean_score = (summed[0, channels, 0] + summed[0, channels + 1, 0]) / (scales * channels * own * bands)
    return (mean_score, decoder_grad, hidden_grad)


def solution(mesh):
    placed = (P("member", "band", None), P(), P(), P(), P(), P(None, "band"), P())
    return jax.shard_map(
        functools.partial(local, dict(mesh.shape)),
        mesh=mesh,
        in_specs=placed,
        out_specs=(P(), P(), P("member", "band", None)),
        check_vma=False,
    )
```

```python
import functools
import math

import jax
import jax.numpy as jnp
from jax import lax
from jax.experimental import pallas as pl
from jax.experimental.pallas import tpu as pltpu
from jax.sharding import PartitionSpec as P

WIN = 128
RMAX = 16
MARGIN = 2 * RMAX
HALO = WIN + MARGIN
LANES = 128
KEYS = 3 * LANES
EDGE = HALO
SUB = EDGE // 2
FRAME = EDGE + 2 * WIN
SCORE_ROWS = 144
SOFT = 0.1 * 0.1
F32 = jnp.float32
BF16 = jnp.bfloat16
NEG = -1e30
NT = (((1,), (1,)), ((), ()))
TN = (((0,), (0,)), ((), ()))


def mm(a, b):
    return jnp.dot(a, b, preferred_element_type=F32)


def half_masks():
    lane = lax.broadcasted_iota(jnp.int32, (1, LANES), 1)
    low = jnp.where(lane < LANES // 2, 1.0, 0.0).astype(BF16)
    return low, (1.0 - low.astype(F32)).astype(BF16)


def put_keys(kz, m, p, rows, piece):
    for h, mask in enumerate(half_masks()):
        kz[m, p, h, rows, :] = piece * mask


def put_values(vz, m, p, rows, piece):
    for h, mask in enumerate(half_masks()):
        vz[m, p, h, rows, :LANES] = piece * mask


def put_ones(vz, pairs):
    shape = vz.shape[:2] + vz.shape[3:4] + (LANES,)
    for h, mask in enumerate(half_masks()):
        vz[:, :, h, :, LANES:] = jnp.broadcast_to(mask.reshape(1, 1, 1, LANES), shape)


def distances(offset):
    qpos = lax.broadcasted_iota(jnp.int32, (WIN, KEYS), 0) + offset
    return jnp.abs(qpos - lax.broadcasted_iota(jnp.int32, (WIN, KEYS), 1))


def take(ref, *at):
    return ref[at]


def keep(ref, m, rows, lanes, values):
    ref[m, rows, lanes] = values


def attend_all(blocks, kz, vz):
    def score(block):
        q, m, p, start = block[:4]
        window = pl.ds(start, KEYS)
        keys = jnp.concatenate([kz[m, p, 0, window, :], kz[m, p, 1, window, :]], axis=0)
        return lax.dot_general(q(), keys, NT, preferred_element_type=F32)

    def soften(logits, block):
        away, reach = block[4](), block[5]
        parts = []
        for h in range(2):
            one = jnp.where(away <= reach[h], logits[:, h * KEYS : (h + 1) * KEYS], NEG)
            peak = jnp.max(one, axis=1, keepdims=True)
            parts.append(jnp.exp(one - peak).astype(BF16))
        return jnp.concatenate(parts, axis=1)

    def finish(probs, block):
        m, p, start = block[1:4]
        window = pl.ds(start, KEYS)
        values = jnp.concatenate([vz[m, p, 0, window, :], vz[m, p, 1, window, :]], axis=0)
        mixed = mm(probs, values)
        block[6]((mixed[:, :LANES] / mixed[:, LANES:]).astype(BF16))

    logits = score(blocks[0])
    probs = None
    for i, block in enumerate(blocks):
        following = score(blocks[i + 1]) if i + 1 < len(blocks) else None
        if probs is not None:
            finish(probs, blocks[i - 1])
        probs = soften(logits, block)
        logits = following
    finish(probs, blocks[-1])


def main_kernel(scale, info, x, xh, wq, wk, wv, wo, dec, q_out, k_out, v_out, hid, fc, kz, vz, qs, att, res, far):
    step = pl.program_id(0)
    members, own, width = x.shape
    cols = wq.shape[1]
    pairs = cols // LANES
    core = info[0]
    lower = core == 1
    halo_at = jnp.where(lower, 0, HALO + own)
    near = jnp.where(lower, WIN, 0)
    edge = jnp.where(lower, 0, own - WIN + MARGIN)

    @pl.when(step == 0)
    def _():
        put_ones(vz, pairs)
        for b in range(2):
            far[b] = distances(WIN + b * (SUB + KEYS - FRAME))

    flat = x[...].reshape(members * own, width)
    flat_halo = xh[...].reshape(members * HALO, width)
    k_own = mm(flat, wk[...]).astype(BF16)
    k_halo = mm(flat_halo, wk[...]).astype(BF16)
    v_own = mm(flat, wv[...]).astype(BF16)
    v_halo = mm(flat_halo, wv[...]).astype(BF16)
    q_own = mm(flat, wq[...]).astype(BF16)
    near_rows = jnp.concatenate(
        [xh[m, pl.ds(pl.multiple_of(near, 32), MARGIN), :] for m in range(members)], axis=0
    )
    q_halo = mm(near_rows, wq[...]).astype(BF16)
    k_out[...] = k_own.reshape(members, own, cols)
    v_out[...] = v_own.reshape(members, own, cols)
    q_own = (q_own.astype(F32) * scale).astype(BF16)
    q_halo = (q_halo.astype(F32) * scale).astype(BF16)
    q_out[...] = q_own.reshape(members, own, cols)
    own_rows = pl.ds(HALO, own)
    halo_rows = pl.ds(pl.multiple_of(halo_at, 32), HALO)
    q_at = pl.ds(pl.multiple_of(halo_at + near, 32), MARGIN)
    for m in range(members):
        qs[m, own_rows, :] = q_own[m * own : (m + 1) * own]
        qs[m, q_at, :] = q_halo[m * MARGIN : (m + 1) * MARGIN]
        for p in range(pairs):
            lanes = slice(p * LANES, (p + 1) * LANES)
            put_keys(kz, m, p, own_rows, k_own[m * own : (m + 1) * own, lanes])
            put_keys(kz, m, p, halo_rows, k_halo[m * HALO : (m + 1) * HALO, lanes])
            put_values(vz, m, p, own_rows, v_own[m * own : (m + 1) * own, lanes])
            put_values(vz, m, p, halo_rows, v_halo[m * HALO : (m + 1) * HALO, lanes])

    inner = own - 2 * WIN
    blocks = []
    for p in range(pairs):
        reach = [info[4 + (step * pairs + p) * 2 + h] for h in range(2)]
        lanes = slice(p * LANES, (p + 1) * LANES)
        out_lanes = pl.ds(pl.multiple_of(step * cols + p * LANES, LANES), LANES)
        for m in range(members):

            for b in range(inner // WIN):
                first = HALO + WIN + b * WIN
                blocks.append(
                    (
                        functools.partial(take, qs, m, pl.ds(first, WIN), lanes),
                        m,
                        p,
                        first - WIN,
                        functools.partial(take, far, 0, slice(None), slice(None)),
                        reach,
                        functools.partial(keep, att, m, pl.ds(b * WIN, WIN), out_lanes),
                    )
                )
            for b in range(2):
                blocks.append(
                    (
                        functools.partial(take, qs, m, pl.ds(pl.multiple_of(edge + WIN + b * SUB, 16), SUB), lanes),
                        m,
                        p,
                        pl.multiple_of(edge + b * (FRAME - KEYS), 32),
                        functools.partial(take, far, b, slice(0, SUB), slice(None)),
                        reach,
                        functools.partial(keep, att, m, pl.ds(inner + b * SUB, SUB), out_lanes),
                    )
                )
    attend_all(blocks, kz, vz)

    @pl.when(step == pl.num_programs(0) - 1)
    def _():
        own_first = jnp.where(lower, MARGIN, 0)
        from_own = pl.ds(pl.multiple_of(jnp.where(lower, 0, own - WIN), 32), WIN)
        for m in range(members):
            res[pl.ds(pl.multiple_of(own_first, 32), WIN), :] = x[m, from_own, :]
            res[pl.ds(pl.multiple_of(jnp.where(lower, 0, WIN), 32), MARGIN), :] = xh[
                m, pl.ds(pl.multiple_of(near, 32), MARGIN), :
            ]
            mixed = mm(att[m], wo[...])
            hid[m, :inner, :] = (mixed[:inner] + x[m, WIN : own - WIN, :].astype(F32)).astype(BF16)
            hid[m, inner:, :] = (mixed[inner:] + res[...].astype(F32)).astype(BF16)
            fc[m] = lax.dot_general(hid[m], dec[...], NT, preferred_element_type=F32)


def edge_kernel(scale, info, x, xh, wq, wk, wv, qi, ki, vi, wo, dec, hid, fc, kz, vz, qs, att, res, far):
    step = pl.program_id(0)
    members, own, width = x.shape
    cols = wq.shape[1]
    pairs = cols // LANES
    lower = info[0] == 0
    halo_at = jnp.where(lower, 0, 2 * WIN)
    own_at = jnp.where(lower, HALO, 0)
    near = jnp.where(lower, WIN, 0)
    low = jnp.where(info[1] == 1, HALO, 0)
    high = jnp.where(info[2] == 1, 2 * WIN, FRAME)

    @pl.when(step == 0)
    def _():
        put_ones(vz, pairs)
        for b in range(2):
            start = b * (FRAME - KEYS)
            kpos = lax.broadcasted_iota(jnp.int32, (WIN, KEYS), 1) + start
            away = distances(WIN + b * SUB - start)
            far[b] = jnp.where((kpos >= low) & (kpos < high), away, 1 << 20)

    flat_halo = xh[...].reshape(members * HALO, width)
    k_halo = mm(flat_halo, wk[...]).astype(BF16)
    v_halo = mm(flat_halo, wv[...]).astype(BF16)
    near_rows = jnp.concatenate(
        [xh[m, pl.ds(pl.multiple_of(near, 32), MARGIN), :] for m in range(members)], axis=0
    )
    q_halo = mm(near_rows, wq[...]).astype(BF16)
    q_halo = (q_halo.astype(F32) * scale).astype(BF16)
    own_rows = pl.ds(pl.multiple_of(own_at, 32), 2 * WIN)
    halo_rows = pl.ds(pl.multiple_of(halo_at, 32), HALO)
    for m in range(members):
        qs[m, pl.ds(pl.multiple_of(jnp.where(lower, MARGIN, 0), 32), WIN), :] = qi[m]
        qs[m, pl.ds(pl.multiple_of(jnp.where(lower, 0, WIN), 32), MARGIN), :] = q_halo[
            m * MARGIN : (m + 1) * MARGIN
        ]
        for p in range(pairs):
            lanes = slice(p * LANES, (p + 1) * LANES)
            put_keys(kz, m, p, own_rows, ki[m, :, lanes])
            put_keys(kz, m, p, halo_rows, k_halo[m * HALO : (m + 1) * HALO, lanes])
            put_values(vz, m, p, own_rows, vi[m, :, lanes])
            put_values(vz, m, p, halo_rows, v_halo[m * HALO : (m + 1) * HALO, lanes])

    blocks = []
    for p in range(pairs):
        reach = [info[4 + (step * pairs + p) * 2 + h] for h in range(2)]
        lanes = slice(p * LANES, (p + 1) * LANES)
        out_lanes = pl.ds(pl.multiple_of(step * cols + p * LANES, LANES), LANES)
        for m in range(members):
            for b in range(2):
                blocks.append(
                    (
                        functools.partial(take, qs, m, pl.ds(b * SUB, SUB), lanes),
                        m,
                        p,
                        b * (FRAME - KEYS),
                        functools.partial(take, far, b, slice(0, SUB), slice(None)),
                        reach,
                        functools.partial(keep, att, m, pl.ds(b * SUB, SUB), out_lanes),
                    )
                )
    attend_all(blocks, kz, vz)

    @pl.when(step == pl.num_programs(0) - 1)
    def _():
        from_own = pl.ds(pl.multiple_of(jnp.where(lower, 0, own - WIN), 32), WIN)
        for m in range(members):
            res[m, pl.ds(pl.multiple_of(jnp.where(lower, MARGIN, 0), 32), WIN), :] = x[m, from_own, :]
            res[m, pl.ds(pl.multiple_of(jnp.where(lower, 0, WIN), 32), MARGIN), :] = xh[
                m, pl.ds(pl.multiple_of(near, 32), MARGIN), :
            ]
        mixed = mm(att[...].reshape(members * EDGE, width), wo[...])
        hidden = (mixed + res[...].reshape(members * EDGE, width).astype(F32)).astype(BF16)
        hid[...] = hidden.reshape(members, EDGE, width)
        fc[...] = lax.dot_general(hidden, dec[...], NT, preferred_element_type=F32).reshape(
            members, EDGE, dec.shape[0]
        )


def toeplitz(radii, scale_index, rows, cols):
    reach = radii[scale_index].astype(F32)
    spread = 0.5 * reach
    twice = 2.0 * spread * spread

    def weigh(shape, shift):
        away = lax.broadcasted_iota(jnp.int32, shape, 1) - shift
        far = jnp.abs(away).astype(F32)
        return jnp.where(far <= reach, jnp.exp(-(far * far) / twice), 0.0)

    line = weigh((8, LANES), RMAX)
    total = jnp.sum(line, axis=1, keepdims=True)[:1]
    shift = lax.broadcasted_iota(jnp.int32, (rows, cols), 0) + RMAX
    return weigh((rows, cols), shift) / total


def split(values):
    high = values.astype(BF16)
    return high, (values - high.astype(F32)).astype(BF16)


def score_kernel(
    channels, members_total, info, radii, fa, fb, ga, gb, truth, t_near, t_far, hid_a, hid_b, cot, part, fh, fl, sh, sl
):
    members, _, _ = fa.shape
    own = truth.shape[0]
    scales = radii.shape[0]
    inner = own - 2 * WIN
    rows = SCORE_ROWS
    window = 2 * LANES
    lower = info[0] == 0
    begins, ends = info[1] == 1, info[2] == 1
    far_at = pl.ds(pl.multiple_of(jnp.where(lower, 0, inner + EDGE), 32), EDGE)
    near_at = pl.ds(pl.multiple_of(jnp.where(lower, inner + EDGE, 0), 32), EDGE)
    total_rows = own + 2 * MARGIN

    def put(at, column, values):
        lanes = slice(column * LANES, (column + 1) * LANES)
        fh[at, lanes], fl[at, lanes] = split(values)

    for side, (f_main, f_far) in enumerate(((fa, fb), (ga, gb))):
        for m in range(members):
            column = side * members + m
            put(pl.ds(EDGE, inner), column, f_main[m, :inner, :])
            put(near_at, column, f_main[m, inner:, :])
            put(far_at, column, f_far[m])
    put(pl.ds(MARGIN, own), 2 * members, truth[...])
    put(pl.ds(pl.multiple_of(jnp.where(lower, 0, MARGIN + own), 32), MARGIN), 2 * members, t_far[...])
    put(pl.ds(pl.multiple_of(jnp.where(lower, MARGIN + own, 0), 32), MARGIN), 2 * members, t_near[...])
    for ref in (fh, fl):
        ref[total_rows:, :] = jnp.zeros((ref.shape[0] - total_rows, ref.shape[1]), BF16)

        @pl.when(begins)
        def _():
            ref[:MARGIN, :] = jnp.zeros((MARGIN, ref.shape[1]), BF16)

        @pl.when(ends)
        def _():
            ref[MARGIN + own : total_rows, :] = jnp.zeros((MARGIN, ref.shape[1]), BF16)

    tiles = -(-(own + 2 * RMAX) // rows)
    for ref in (sh, sl):
        spare = ref.shape[1] - tiles * rows
        ref[:, tiles * rows :, :] = jnp.zeros((scales, spare, ref.shape[2]), BF16)

    weights = [split(toeplitz(radii, s, rows, window)) for s in range(scales)]
    forward = jnp.concatenate([jnp.concatenate([h, h, l], axis=1) for h, l in weights], axis=0)
    backward = jnp.concatenate(
        [h[:LANES] for h, l in weights] + [h[:LANES] for h, l in weights] + [l[:LANES] for h, l in weights],
        axis=1,
    )
    first_valid = jnp.where(begins, RMAX, 0)
    last_valid = jnp.where(ends, RMAX + own, 2 * RMAX + own)
    pair_weight = 1.0 / (members_total * (members_total - 1))
    others = 2 * members
    total = jnp.zeros((rows, LANES), F32)
    for tile in range(tiles):
        at = pl.ds(tile * rows, window)
        stacked = jnp.concatenate([fh[at, :], fl[at, :], fh[at, :]], axis=0)
        smooth = mm(forward, stacked)
        line = lax.broadcasted_iota(jnp.int32, (rows, LANES), 0) + tile * rows
        valid = jnp.where((line >= first_valid) & (line < last_valid), 1.0, 0.0)
        tile_score = jnp.zeros((rows, LANES), F32)
        for s in range(scales):
            values = [
                smooth[s * rows : (s + 1) * rows, i * LANES : (i + 1) * LANES] for i in range(others + 1)
            ]

            def gap(a, b):
                away = values[a] - values[b]
                square = away * away + SOFT
                inverse = lax.rsqrt(square)
                return away * inverse, square * inverse

            skill = jnp.zeros((rows, LANES), F32)
            spread = jnp.zeros((rows, LANES), F32)
            slopes = []
            cross = [jnp.zeros((rows, LANES), F32) for _ in range(members)]
            for m in range(members):
                slope, size = gap(m, others)
                skill = skill + size
                slopes.append(slope)
            for a in range(members):
                for b in range(a + 1, others):
                    slope, size = gap(a, b)
                    cross[a] = cross[a] + slope
                    if b < members:
                        cross[b] = cross[b] - slope
                        spread = spread + size
                    else:
                        spread = spread + 0.5 * size
            tile_score = tile_score + (skill * (1.0 / members_total) - pair_weight * spread)
            for m in range(members):
                slope = (slopes[m] * (1.0 / members_total) - pair_weight * cross[m]) * valid
                keep, lanes = pl.ds(tile * rows, rows), slice(m * LANES, (m + 1) * LANES)
                sh[s, keep, lanes], sl[s, keep, lanes] = split(slope)
        mine = (line >= RMAX) & (line < RMAX + own)
        total = total + jnp.where(mine, tile_score, 0.0)
    lane = lax.broadcasted_iota(jnp.int32, (rows, LANES), 1)
    total = jnp.where(lane < channels, total, 0.0)
    score = jnp.sum(jnp.sum(total, axis=0, keepdims=True), axis=1, keepdims=True)

    for tile in range(own // LANES):
        at = pl.ds(tile * LANES, window)
        high = [sh[s, at, :] for s in range(scales)]
        low = [sl[s, at, :] for s in range(scales)]
        stacked = jnp.concatenate(high + low + high, axis=0)
        cot[tile * LANES : (tile + 1) * LANES, :] = mm(backward, stacked).astype(BF16)

    near_own = pl.ds(pl.multiple_of(jnp.where(lower, own - WIN, 0), 32), WIN)
    far_own = pl.ds(pl.multiple_of(jnp.where(lower, 0, own - WIN), 32), WIN)
    near_skip = pl.multiple_of(jnp.where(lower, 0, MARGIN), 32)
    far_skip = pl.multiple_of(jnp.where(lower, MARGIN, 0), 32)
    width = hid_a.shape[2]
    grad = jnp.zeros((LANES, width), F32)
    for m in range(members):
        lanes = slice(m * LANES, (m + 1) * LANES)
        for c_rows, ref, h_rows in (
            (pl.ds(WIN, inner), hid_a, pl.ds(0, inner)),
            (near_own, hid_a, pl.ds(inner + near_skip, WIN)),
            (far_own, hid_b, pl.ds(far_skip, WIN)),
        ):
            grad = grad + lax.dot_general(cot[c_rows, lanes], ref[m, h_rows, :], TN, preferred_element_type=F32)
    chunks = width // LANES // part.shape[0]
    extra = part.shape[1] - chunks * channels
    line = lax.broadcasted_iota(jnp.int32, (extra, LANES), 0)
    score_high = score.astype(BF16).astype(F32)
    tail = jnp.where(line == 0, score_high, jnp.where(line == 1, score - score_high, 0.0)).astype(BF16)
    for h in range(part.shape[0]):
        for c in range(chunks):
            first = (h * chunks + c) * LANES
            part[h, c * channels : (c + 1) * channels, :] = grad[:channels, first : first + LANES].astype(BF16)
        part[h, chunks * channels :, :] = tail


def grad_kernel(cot, dec, out):
    out[0] = mm(cot[...], dec[...]).astype(BF16)


def swap_pairs(count, first):
    pairs = []
    for i in range(first, count - 1, 2):
        pairs += [(i, i + 1), (i + 1, i)]
    return pairs


def reduce_all(part, mesh_shape, beside):
    bands, count = mesh_shape["band"], mesh_shape["member"]
    core = lax.axis_index("band") % 2

    def swap(values, axis, size, bit):
        return lax.ppermute(values, axis, [(i, i ^ bit) for i in range(size)])

    def add(mine, theirs):
        return (mine.astype(F32) + theirs.astype(F32)).astype(BF16)

    theirs = lax.dynamic_index_in_dim(part, 1 - core, 0, keepdims=False)
    mine = lax.dynamic_index_in_dim(part, core, 0, keepdims=False)
    total = add(mine, swap(theirs, "band", bands, 1))
    steps = [("member", count, 1 << i) for i in range(count.bit_length() - 1)]
    steps += [("band", bands, 1 << i) for i in range(1, bands.bit_length() - 1)]
    aside = None
    for i, (axis, size, bit) in enumerate(steps):
        got = swap(total, axis, size, bit)
        if i == 0:
            aside = beside(total)
            got, aside = lax.optimization_barrier((got, aside))
        total = add(total, got)
    other = swap(total, "band", bands, 1)
    low = jnp.where(core == 0, total, other)
    high = jnp.where(core == 0, other, total)
    return jnp.stack([low, high]).astype(F32), aside


def local(mesh_shape, fields, w_qkv, w_out, decoder_weight, window_reach, truth, radii):
    members, own, width = fields.shape
    heads = window_reach.shape[0]
    head = width // heads
    channels = decoder_weight.shape[0]
    scales = radii.shape[0]
    bands, member_count = mesh_shape["band"], mesh_shape["member"]
    members_total = members * member_count
    scale = head**-0.5
    band = lax.axis_index("band")
    core = band % 2
    info = jnp.concatenate(
        [
            jnp.stack([core, band == 0, band == bands - 1, 0]).astype(jnp.int32),
            window_reach.astype(jnp.int32),
        ]
    )
    inside = swap_pairs(bands, 0)
    across = swap_pairs(bands, 1) + [(0, 0), (bands - 1, bands - 1)]

    def exchange(block, dim, size):
        last = block.shape[dim] - size
        near = lax.dynamic_slice_in_dim(block, (1 - core) * last, size, dim)
        far = lax.dynamic_slice_in_dim(block, core * last, size, dim)
        return lax.ppermute(near, "band", inside), lax.ppermute(far, "band", across)

    x_near, x_far = exchange(fields, 1, HALO)
    truth_t = jnp.pad(truth.T, ((0, 0), (0, LANES - channels)))
    t_near, t_far = exchange(truth_t, 0, MARGIN)
    dec = jnp.pad(decoder_weight, ((0, LANES - channels), (0, 0)))

    cols = 2 * LANES
    steps = width // cols
    pairs = cols // LANES
    whole = lambda shape: pl.BlockSpec(shape, lambda i, s: (0,) * len(shape))
    weight = lambda third: pl.BlockSpec((width, cols), lambda i, s: (0, third * steps + i))
    inner = own - 2 * WIN
    main_rows = inner + EDGE
    col_block = lambda rows: pl.BlockSpec((members, rows, cols), lambda i, s: (0, 0, i))
    params = pltpu.CompilerParams(
        dimension_semantics=("arbitrary",), vmem_limit_bytes=48 * 1024 * 1024
    )
    q_own, k_own, v_own, hid_a, fc_a = pl.pallas_call(
        functools.partial(main_kernel, scale),
        grid_spec=pltpu.PrefetchScalarGridSpec(
            num_scalar_prefetch=1,
            grid=(steps,),
            in_specs=[
                whole((members, own, width)),
                whole((members, HALO, width)),
                weight(0),
                weight(1),
                weight(2),
                whole((width, width)),
                whole((LANES, width)),
            ],
            out_specs=[
                col_block(own),
                col_block(own),
                col_block(own),
                whole((members, main_rows, width)),
                whole((members, main_rows, LANES)),
            ],
            scratch_shapes=[
                pltpu.VMEM((members, pairs, 2, own + 2 * HALO, LANES), BF16),
                pltpu.VMEM((members, pairs, 2, own + 2 * HALO, 2 * LANES), BF16),
                pltpu.VMEM((members, own + 2 * HALO, cols), BF16),
                pltpu.VMEM((members, main_rows, width), BF16),
                pltpu.VMEM((EDGE, width), BF16),
                pltpu.VMEM((2, WIN, KEYS), jnp.int32),
            ],
        ),
        out_shape=[jax.ShapeDtypeStruct((members, own, width), BF16)] * 3
        + [
            jax.ShapeDtypeStruct((members, main_rows, width), BF16),
            jax.ShapeDtypeStruct((members, main_rows, LANES), F32),
        ],
        compiler_params=params,
        cost_estimate=pl.CostEstimate(
            flops=2 * members * own * width * 5 * width, bytes_accessed=24 << 20, transcendentals=1 << 22
        ),
    )(info, fields, x_near, w_qkv, w_qkv, w_qkv, w_out, dec)

    member_pairs = [(i, i ^ 1) for i in range(member_count)]
    other_a = lax.ppermute(fc_a, "member", member_pairs)

    far_block = lambda rows, last: pl.BlockSpec((members, rows, cols), lambda i, s: (0, s[0] * last, i))
    hid_b, fc_b = pl.pallas_call(
        functools.partial(edge_kernel, scale),
        grid_spec=pltpu.PrefetchScalarGridSpec(
            num_scalar_prefetch=1,
            grid=(steps,),
            in_specs=[
                whole((members, own, width)),
                whole((members, HALO, width)),
                weight(0),
                weight(1),
                weight(2),
                far_block(WIN, own // WIN - 1),
                far_block(2 * WIN, own // (2 * WIN) - 1),
                far_block(2 * WIN, own // (2 * WIN) - 1),
                whole((width, width)),
                whole((LANES, width)),
            ],
            out_specs=[whole((members, EDGE, width)), whole((members, EDGE, LANES))],
            scratch_shapes=[
                pltpu.VMEM((members, pairs, 2, FRAME, LANES), BF16),
                pltpu.VMEM((members, pairs, 2, FRAME, 2 * LANES), BF16),
                pltpu.VMEM((members, EDGE, cols), BF16),
                pltpu.VMEM((members, EDGE, width), BF16),
                pltpu.VMEM((members, EDGE, width), BF16),
                pltpu.VMEM((2, WIN, KEYS), jnp.int32),
            ],
        ),
        out_shape=[
            jax.ShapeDtypeStruct((members, EDGE, width), BF16),
            jax.ShapeDtypeStruct((members, EDGE, LANES), F32),
        ],
        compiler_params=params,
        cost_estimate=pl.CostEstimate(
            flops=2 * members * own * width * 2 * width, bytes_accessed=14 << 20, transcendentals=1 << 21
        ),
    )(info, fields, x_far, w_qkv, w_qkv, w_qkv, q_own, k_own, v_own, w_out, dec)
    other_b = lax.ppermute(fc_b, "member", member_pairs)

    chunks = width // LANES // 2
    keep_rows = chunks * channels + 16
    tiles = -(-(own + 2 * RMAX) // SCORE_ROWS)
    f_rows = (tiles - 1) * SCORE_ROWS + 2 * LANES
    s_rows = own + LANES
    smem = pl.BlockSpec(memory_space=pltpu.SMEM)
    vmem = pl.BlockSpec(memory_space=pltpu.VMEM)
    cot, part = pl.pallas_call(
        functools.partial(score_kernel, channels, members_total),
        in_specs=[smem, smem] + [vmem] * 9,
        out_specs=[vmem, vmem],
        out_shape=[
            jax.ShapeDtypeStruct((own, members * LANES), BF16),
            jax.ShapeDtypeStruct((2, keep_rows, LANES), BF16),
        ],
        scratch_shapes=[
            pltpu.VMEM((f_rows, (2 * members + 1) * LANES), BF16),
            pltpu.VMEM((f_rows, (2 * members + 1) * LANES), BF16),
            pltpu.VMEM((scales, s_rows, members * LANES), BF16),
            pltpu.VMEM((scales, s_rows, members * LANES), BF16),
        ],
        compiler_params=pltpu.CompilerParams(vmem_limit_bytes=48 * 1024 * 1024),
    )(info, radii, fc_a, fc_b, other_a, other_b, truth_t, t_near, t_far, hid_a, hid_b)

    def pull_back(sent):
        cot_now, _ = lax.optimization_barrier((cot, sent))
        return pl.pallas_call(
            grad_kernel,
            grid=(members, 2),
            in_specs=[
                pl.BlockSpec((own // 2, LANES), lambda m, h: (h, m)),
                pl.BlockSpec((LANES, width), lambda m, h: (0, 0)),
            ],
            out_specs=pl.BlockSpec((1, own // 2, width), lambda m, h: (m, h, 0)),
            out_shape=jax.ShapeDtypeStruct((members, own, width), BF16),
            cost_estimate=pl.CostEstimate(
                flops=2 * members * own * LANES * width, bytes_accessed=8 << 20, transcendentals=0
            ),
        )(cot_now, dec)

    summed, hidden_grad = reduce_all(part, mesh_shape, pull_back)
    decoder_grad = summed[:, : chunks * channels].reshape(2 * chunks, channels, LANES)
    decoder_grad = decoder_grad.transpose(1, 0, 2).reshape(channels, width)
    decoder_grad = decoder_grad / math.sqrt(members_total * own * bands)
    score = summed[0, chunks * channels, 0] + summed[0, chunks * channels + 1, 0]
    mean_score = score / (scales * channels * own * bands)
    return (mean_score, decoder_grad, hidden_grad)


def solution(mesh):
    placed = (P("member", "band", None), P(), P(), P(), P(), P(None, "band"), P())
    return jax.shard_map(
        functools.partial(local, dict(mesh.shape)),
        mesh=mesh,
        in_specs=placed,
        out_specs=(P(), P(), P("member", "band", None)),
        check_vma=False,
    )
```

```python
import functools
import math

import jax
import jax.numpy as jnp
from jax import lax
from jax.experimental import pallas as pl
from jax.experimental.pallas import tpu as pltpu
from jax.sharding import PartitionSpec as P

WIN = 128
RMAX = 16
MARGIN = 2 * RMAX
HALO = WIN + MARGIN
LANES = 128
KEYS = 3 * LANES
EDGE = HALO
SUB = EDGE // 2
FRAME = EDGE + 2 * WIN
SCORE_ROWS = 144
CHUNK = 512
SOFT = 0.1 * 0.1
F32 = jnp.float32
BF16 = jnp.bfloat16
NEG = -1e30
NT = (((1,), (1,)), ((), ()))
TN = (((0,), (0,)), ((), ()))


def mm(a, b):
    return jnp.dot(a, b, preferred_element_type=F32)


def half_masks():
    lane = lax.broadcasted_iota(jnp.int32, (1, LANES), 1)
    low = jnp.where(lane < LANES // 2, 1.0, 0.0).astype(BF16)
    return low, (1.0 - low.astype(F32)).astype(BF16)


def put_keys(kz, m, p, rows, piece):
    for h, mask in enumerate(half_masks()):
        kz[m, p, h, rows, :] = piece * mask


def put_values(vz, m, p, rows, piece):
    for h, mask in enumerate(half_masks()):
        vz[m, p, h, rows, :LANES] = piece * mask


def put_ones(vz, pairs):
    shape = vz.shape[:2] + vz.shape[3:4] + (LANES,)
    for h, mask in enumerate(half_masks()):
        vz[:, :, h, :, LANES:] = jnp.broadcast_to(mask.reshape(1, 1, 1, LANES), shape)


def distances(offset):
    qpos = lax.broadcasted_iota(jnp.int32, (WIN, KEYS), 0) + offset
    return jnp.abs(qpos - lax.broadcasted_iota(jnp.int32, (WIN, KEYS), 1))


def take(ref, *at):
    return ref[at]


def keep(ref, m, rows, lanes, values):
    ref[m, rows, lanes] = values


def attend_all(blocks, kz, vz, beside=()):
    def score(block):
        q, m, p, start = block[:4]
        window = pl.ds(start, KEYS)
        keys = jnp.concatenate([kz[m, p, 0, window, :], kz[m, p, 1, window, :]], axis=0)
        return lax.dot_general(q(), keys, NT, preferred_element_type=F32)

    def soften(logits, block):
        away, reach = block[4](), block[5]
        parts = []
        for h in range(2):
            one = jnp.where(away <= reach[h], logits[:, h * KEYS : (h + 1) * KEYS], NEG)
            peak = jnp.max(one, axis=1, keepdims=True)
            parts.append(jnp.exp(one - peak).astype(BF16))
        return jnp.concatenate(parts, axis=1)

    def finish(probs, block):
        m, p, start = block[1:4]
        window = pl.ds(start, KEYS)
        values = jnp.concatenate([vz[m, p, 0, window, :], vz[m, p, 1, window, :]], axis=0)
        mixed = mm(probs, values)
        block[6]((mixed[:, :LANES] / mixed[:, LANES:]).astype(BF16))

    beside = list(beside)
    total = len(beside)
    logits = score(blocks[0])
    probs = None
    for i, block in enumerate(blocks):
        following = score(blocks[i + 1]) if i + 1 < len(blocks) else None
        while beside and len(beside) * len(blocks) > (len(blocks) - 1 - i) * total:
            beside.pop(0)()
        if probs is not None:
            finish(probs, blocks[i - 1])
        probs = soften(logits, block)
        logits = following
    finish(probs, blocks[-1])


def main_kernel(
    scale, info, x, xh, wq, wk, wv, wo_hbm, dec, q_out, k_out, v_out, hid, fc,
    kz0, vz0, qs0, kz1, vz1, qs1, att, res, far, wo, sem,
):
    step = pl.program_id(0)
    members, own, width = x.shape
    cols = wq.shape[1]
    pairs = cols // LANES
    groups = width // cols
    sets = ((kz0, vz0, qs0), (kz1, vz1, qs1))
    lower = info[0] == 1
    halo_at = jnp.where(lower, 0, HALO + own)
    near = jnp.where(lower, WIN, 0)
    edge = jnp.where(lower, 0, own - WIN + MARGIN)
    halo_rows = pl.ds(pl.multiple_of(halo_at, 32), HALO)
    near_from = pl.ds(pl.multiple_of(near, 32), MARGIN)
    near_at = pl.ds(pl.multiple_of(halo_at + near, 32), MARGIN)
    inner = own - 2 * WIN
    weight_copy = pltpu.make_async_copy(wo_hbm, wo, sem)

    def own_chunk(kind, m, first, rows, kz, vz, qs):
        weight = (wq, wk, wv)[kind]
        at, to = pl.ds(first, rows), pl.ds(HALO + first, rows)
        made = mm(x[m, at, :], weight[...]).astype(BF16)
        if kind == 0:
            made = (made.astype(F32) * scale).astype(BF16)
            qs[m, to, :] = made
        else:
            for p in range(pairs):
                put = (put_keys, put_values)[kind - 1]
                put((kz, vz)[kind - 1], m, p, to, made[:, p * LANES : (p + 1) * LANES])
        (q_out, k_out, v_out)[kind][m, at, :] = made

    def halo_chunk(kind, kz, vz):
        made = mm(xh[...].reshape(members * HALO, width), (wk, wv)[kind][...]).astype(BF16)
        for m in range(members):
            for p in range(pairs):
                put = (put_keys, put_values)[kind]
                put((kz, vz)[kind], m, p, halo_rows, made[m * HALO : (m + 1) * HALO, p * LANES : (p + 1) * LANES])

    def near_chunk(qs):
        rows = jnp.concatenate([xh[m, near_from, :] for m in range(members)], axis=0)
        made = (mm(rows, wq[...]).astype(BF16).astype(F32) * scale).astype(BF16)
        for m in range(members):
            qs[m, near_at, :] = made[m * MARGIN : (m + 1) * MARGIN]

    def projections(kz, vz, qs):
        todo = []
        for kind in (1, 2, 0):
            for m in range(members):
                for first in range(0, own, CHUNK):
                    todo.append(functools.partial(own_chunk, kind, m, first, CHUNK, kz, vz, qs))
            todo.append(functools.partial(halo_chunk, kind - 1, kz, vz) if kind else functools.partial(near_chunk, qs))
        return todo

    def attention(group, kz, vz, qs, beside=()):
        blocks = []
        for p in range(pairs):
            reach = [info[4 + (group * pairs + p) * 2 + h] for h in range(2)]
            lanes = slice(p * LANES, (p + 1) * LANES)
            out_lanes = pl.ds(pl.multiple_of(group * cols + p * LANES, LANES), LANES)
            for m in range(members):
                for b in range(inner // WIN):
                    first = HALO + WIN + b * WIN
                    blocks.append(
                        (
                            functools.partial(take, qs, m, pl.ds(first, WIN), lanes),
                            m,
                            p,
                            first - WIN,
                            functools.partial(take, far, 0, slice(None), slice(None)),
                            reach,
                            functools.partial(keep, att, m, pl.ds(b * WIN, WIN), out_lanes),
                        )
                    )
                for b in range(2):
                    q_rows = pl.ds(pl.multiple_of(edge + WIN + b * SUB, 16), SUB)
                    blocks.append(
                        (
                            functools.partial(take, qs, m, q_rows, lanes),
                            m,
                            p,
                            pl.multiple_of(edge + b * (FRAME - KEYS), 32),
                            functools.partial(take, far, b, slice(0, SUB), slice(None)),
                            reach,
                            functools.partial(keep, att, m, pl.ds(inner + b * SUB, SUB), out_lanes),
                        )
                    )
        attend_all(blocks, kz, vz, beside)

    @pl.when(step == 0)
    def _():
        weight_copy.start()
        for _, vz, _ in sets:
            put_ones(vz, pairs)
        for b in range(2):
            far[b] = distances(WIN + b * (SUB + KEYS - FRAME))
        for work in projections(*sets[0]):
            work()

    for parity in range(2):

        @pl.when((step > 0) & (step < groups) & (step % 2 == parity))
        def _():
            attention(step - 1, *sets[1 - parity], beside=projections(*sets[parity]))

    @pl.when(step == groups)
    def _():
        attention(step - 1, *sets[(groups - 1) % 2])
        weight_copy.wait()
        own_first = jnp.where(lower, MARGIN, 0)
        from_own = pl.ds(pl.multiple_of(jnp.where(lower, 0, own - WIN), 32), WIN)
        for m in range(members):
            res[pl.ds(pl.multiple_of(own_first, 32), WIN), :] = x[m, from_own, :]
            res[pl.ds(pl.multiple_of(jnp.where(lower, 0, WIN), 32), MARGIN), :] = xh[m, near_from, :]
            mixed = mm(att[m], wo[...])
            hid[m, :inner, :] = (mixed[:inner] + x[m, WIN : own - WIN, :].astype(F32)).astype(BF16)
            hid[m, inner:, :] = (mixed[inner:] + res[...].astype(F32)).astype(BF16)
            fc[m] = lax.dot_general(hid[m], dec[...], NT, preferred_element_type=F32)


def edge_kernel(
    scale, info, x, xh, wq, wk, wv, qi, ki, vi, wo_hbm, dec, hid, fc, kz0, vz0, qs0, kz1, vz1, qs1, att, res, far, wo, sem
):
    step = pl.program_id(0)
    members, _, width = x.shape
    cols = wq.shape[1]
    pairs = cols // LANES
    groups = width // cols
    sets = ((kz0, vz0, qs0), (kz1, vz1, qs1))
    lower = info[0] == 0
    own_rows = pl.ds(pl.multiple_of(jnp.where(lower, HALO, 0), 32), 2 * WIN)
    halo_rows = pl.ds(pl.multiple_of(jnp.where(lower, 0, 2 * WIN), 32), HALO)
    near_from = pl.ds(pl.multiple_of(jnp.where(lower, WIN, 0), 32), MARGIN)
    own_at = pl.ds(pl.multiple_of(jnp.where(lower, MARGIN, 0), 32), WIN)
    near_at = pl.ds(pl.multiple_of(jnp.where(lower, 0, WIN), 32), MARGIN)
    low = jnp.where(info[1] == 1, HALO, 0)
    high = jnp.where(info[2] == 1, 2 * WIN, FRAME)
    weight_copy = pltpu.make_async_copy(wo_hbm, wo, sem)

    def own_chunk(kind, m, p, target):
        lanes = slice(p * LANES, (p + 1) * LANES)
        (put_keys, put_values)[kind](target, m, p, own_rows, (ki, vi)[kind][m, :, lanes])

    def halo_chunk(kind, m, kz, vz):
        made = mm(xh[m], (wk, wv)[kind][...]).astype(BF16)
        for p in range(pairs):
            (put_keys, put_values)[kind]((kz, vz)[kind], m, p, halo_rows, made[:, p * LANES : (p + 1) * LANES])

    def query_chunk(qs):
        rows = jnp.concatenate([xh[m, near_from, :] for m in range(members)], axis=0)
        made = (mm(rows, wq[...]).astype(BF16).astype(F32) * scale).astype(BF16)
        for m in range(members):
            qs[m, own_at, :] = qi[m]
            qs[m, near_at, :] = made[m * MARGIN : (m + 1) * MARGIN]

    def projections(kz, vz, qs):
        todo = []
        for kind in range(2):
            for m in range(members):
                todo.append(functools.partial(halo_chunk, kind, m, kz, vz))
                for p in range(pairs):
                    todo.append(functools.partial(own_chunk, kind, m, p, (kz, vz)[kind]))
        todo.append(functools.partial(query_chunk, qs))
        return todo

    def attention(group, kz, vz, qs, beside=()):
        blocks = []
        for p in range(pairs):
            reach = [info[4 + (group * pairs + p) * 2 + h] for h in range(2)]
            lanes = slice(p * LANES, (p + 1) * LANES)
            out_lanes = pl.ds(pl.multiple_of(group * cols + p * LANES, LANES), LANES)
            for m in range(members):
                for b in range(2):
                    blocks.append(
                        (
                            functools.partial(take, qs, m, pl.ds(b * SUB, SUB), lanes),
                            m,
                            p,
                            b * (FRAME - KEYS),
                            functools.partial(take, far, b, slice(0, SUB), slice(None)),
                            reach,
                            functools.partial(keep, att, m, pl.ds(b * SUB, SUB), out_lanes),
                        )
                    )
        attend_all(blocks, kz, vz, beside)

    @pl.when(step == 0)
    def _():
        weight_copy.start()
        for _, vz, _ in sets:
            put_ones(vz, pairs)
        for b in range(2):
            start = b * (FRAME - KEYS)
            kpos = lax.broadcasted_iota(jnp.int32, (WIN, KEYS), 1) + start
            away = distances(WIN + b * SUB - start)
            far[b] = jnp.where((kpos >= low) & (kpos < high), away, 1 << 20)
        for work in projections(*sets[0]):
            work()

    for parity in range(2):

        @pl.when((step > 0) & (step < groups) & (step % 2 == parity))
        def _():
            attention(step - 1, *sets[1 - parity], beside=projections(*sets[parity]))

    @pl.when(step == groups)
    def _():
        attention(step - 1, *sets[(groups - 1) % 2])
        weight_copy.wait()
        for m in range(members):
            res[m, own_at, :] = x[m]
            res[m, near_at, :] = xh[m, near_from, :]
        mixed = mm(att[...].reshape(members * EDGE, width), wo[...])
        hidden = (mixed + res[...].reshape(members * EDGE, width).astype(F32)).astype(BF16)
        hid[...] = hidden.reshape(members, EDGE, width)
        fc[...] = lax.dot_general(hidden, dec[...], NT, preferred_element_type=F32).reshape(
            members, EDGE, dec.shape[0]
        )


def toeplitz(radii, scale_index, rows, cols):
    reach = radii[scale_index].astype(F32)
    spread = 0.5 * reach
    twice = 2.0 * spread * spread

    def weigh(shape, shift):
        away = lax.broadcasted_iota(jnp.int32, shape, 1) - shift
        far = jnp.abs(away).astype(F32)
        return jnp.where(far <= reach, jnp.exp(-(far * far) / twice), 0.0)

    line = weigh((8, LANES), RMAX)
    total = jnp.sum(line, axis=1, keepdims=True)[:1]
    shift = lax.broadcasted_iota(jnp.int32, (rows, cols), 0) + RMAX
    return weigh((rows, cols), shift) / total


def split(values):
    high = values.astype(BF16)
    return high, (values - high.astype(F32)).astype(BF16)


def score_kernel(
    channels, members_total, info, radii, fa, fb, ga, gb, truth, t_near, t_far, hid_a, hid_b, cot, part, fh, fl, sh, sl
):
    members, _, _ = fa.shape
    own = truth.shape[0]
    scales = radii.shape[0]
    inner = own - 2 * WIN
    rows = SCORE_ROWS
    window = 2 * LANES
    lower = info[0] == 0
    begins, ends = info[1] == 1, info[2] == 1
    far_at = pl.ds(pl.multiple_of(jnp.where(lower, 0, inner + EDGE), 32), EDGE)
    near_at = pl.ds(pl.multiple_of(jnp.where(lower, inner + EDGE, 0), 32), EDGE)
    total_rows = own + 2 * MARGIN

    def put(at, column, values):
        lanes = slice(column * LANES, (column + 1) * LANES)
        fh[at, lanes], fl[at, lanes] = split(values)

    for side, (f_main, f_far) in enumerate(((fa, fb), (ga, gb))):
        for m in range(members):
            column = side * members + m
            put(pl.ds(EDGE, inner), column, f_main[m, :inner, :])
            put(near_at, column, f_main[m, inner:, :])
            put(far_at, column, f_far[m])
    put(pl.ds(MARGIN, own), 2 * members, truth[...])
    put(pl.ds(pl.multiple_of(jnp.where(lower, 0, MARGIN + own), 32), MARGIN), 2 * members, t_far[...])
    put(pl.ds(pl.multiple_of(jnp.where(lower, MARGIN + own, 0), 32), MARGIN), 2 * members, t_near[...])
    for ref in (fh, fl):
        ref[total_rows:, :] = jnp.zeros((ref.shape[0] - total_rows, ref.shape[1]), BF16)

        @pl.when(begins)
        def _():
            ref[:MARGIN, :] = jnp.zeros((MARGIN, ref.shape[1]), BF16)

        @pl.when(ends)
        def _():
            ref[MARGIN + own : total_rows, :] = jnp.zeros((MARGIN, ref.shape[1]), BF16)

    tiles = -(-(own + 2 * RMAX) // rows)
    for ref in (sh, sl):
        spare = ref.shape[1] - tiles * rows
        ref[:, tiles * rows :, :] = jnp.zeros((scales, spare, ref.shape[2]), BF16)

    weights = [split(toeplitz(radii, s, rows, window)) for s in range(scales)]
    forward = jnp.concatenate([jnp.concatenate([h, h, l], axis=1) for h, l in weights], axis=0)
    backward = jnp.concatenate(
        [h[:LANES] for h, l in weights] + [h[:LANES] for h, l in weights] + [l[:LANES] for h, l in weights],
        axis=1,
    )
    first_valid = jnp.where(begins, RMAX, 0)
    last_valid = jnp.where(ends, RMAX + own, 2 * RMAX + own)
    pair_weight = 1.0 / (members_total * (members_total - 1))
    others = 2 * members
    total = jnp.zeros((rows, LANES), F32)
    for tile in range(tiles):
        at = pl.ds(tile * rows, window)
        stacked = jnp.concatenate([fh[at, :], fl[at, :], fh[at, :]], axis=0)
        smooth = mm(forward, stacked)
        line = lax.broadcasted_iota(jnp.int32, (rows, LANES), 0) + tile * rows
        valid = jnp.where((line >= first_valid) & (line < last_valid), 1.0, 0.0)
        tile_score = jnp.zeros((rows, LANES), F32)
        for s in range(scales):
            values = [
                smooth[s * rows : (s + 1) * rows, i * LANES : (i + 1) * LANES] for i in range(others + 1)
            ]

            def gap(a, b):
                away = values[a] - values[b]
                square = away * away + SOFT
                inverse = lax.rsqrt(square)
                return away * inverse, square * inverse

            skill = jnp.zeros((rows, LANES), F32)
            spread = jnp.zeros((rows, LANES), F32)
            slopes = []
            cross = [jnp.zeros((rows, LANES), F32) for _ in range(members)]
            for m in range(members):
                slope, size = gap(m, others)
                skill = skill + size
                slopes.append(slope)
            for a in range(members):
                for b in range(a + 1, others):
                    slope, size = gap(a, b)
                    cross[a] = cross[a] + slope
                    if b < members:
                        cross[b] = cross[b] - slope
                        spread = spread + size
                    else:
                        spread = spread + 0.5 * size
            tile_score = tile_score + (skill * (1.0 / members_total) - pair_weight * spread)
            for m in range(members):
                slope = (slopes[m] * (1.0 / members_total) - pair_weight * cross[m]) * valid
                keep, lanes = pl.ds(tile * rows, rows), slice(m * LANES, (m + 1) * LANES)
                sh[s, keep, lanes], sl[s, keep, lanes] = split(slope)
        mine = (line >= RMAX) & (line < RMAX + own)
        total = total + jnp.where(mine, tile_score, 0.0)
    lane = lax.broadcasted_iota(jnp.int32, (rows, LANES), 1)
    total = jnp.where(lane < channels, total, 0.0)
    score = jnp.sum(jnp.sum(total, axis=0, keepdims=True), axis=1, keepdims=True)

    for tile in range(own // LANES):
        at = pl.ds(tile * LANES, window)
        high = [sh[s, at, :] for s in range(scales)]
        low = [sl[s, at, :] for s in range(scales)]
        stacked = jnp.concatenate(high + low + high, axis=0)
        cot[tile * LANES : (tile + 1) * LANES, :] = mm(backward, stacked).astype(BF16)

    near_own = pl.ds(pl.multiple_of(jnp.where(lower, own - WIN, 0), 32), WIN)
    far_own = pl.ds(pl.multiple_of(jnp.where(lower, 0, own - WIN), 32), WIN)
    near_skip = pl.multiple_of(jnp.where(lower, 0, MARGIN), 32)
    far_skip = pl.multiple_of(jnp.where(lower, MARGIN, 0), 32)
    width = hid_a.shape[2]
    grad = jnp.zeros((LANES, width), F32)
    for m in range(members):
        lanes = slice(m * LANES, (m + 1) * LANES)
        for c_rows, ref, h_rows in (
            (pl.ds(WIN, inner), hid_a, pl.ds(0, inner)),
            (near_own, hid_a, pl.ds(inner + near_skip, WIN)),
            (far_own, hid_b, pl.ds(far_skip, WIN)),
        ):
            grad = grad + lax.dot_general(cot[c_rows, lanes], ref[m, h_rows, :], TN, preferred_element_type=F32)
    chunks = width // LANES // part.shape[0]
    extra = part.shape[1] - chunks * channels
    line = lax.broadcasted_iota(jnp.int32, (extra, LANES), 0)
    score_high = score.astype(BF16).astype(F32)
    tail = jnp.where(line == 0, score_high, jnp.where(line == 1, score - score_high, 0.0)).astype(BF16)
    for h in range(part.shape[0]):
        for c in range(chunks):
            first = (h * chunks + c) * LANES
            part[h, c * channels : (c + 1) * channels, :] = grad[:channels, first : first + LANES].astype(BF16)
        part[h, chunks * channels :, :] = tail


def grad_kernel(cot, dec, out):
    out[0] = mm(cot[...], dec[...]).astype(BF16)


def swap_pairs(count, first):
    pairs = []
    for i in range(first, count - 1, 2):
        pairs += [(i, i + 1), (i + 1, i)]
    return pairs


def reduce_all(part, mesh_shape, beside):
    bands, count = mesh_shape["band"], mesh_shape["member"]
    core = lax.axis_index("band") % 2

    def swap(values, axis, size, bit):
        return lax.ppermute(values, axis, [(i, i ^ bit) for i in range(size)])

    def add(mine, theirs):
        return (mine.astype(F32) + theirs.astype(F32)).astype(BF16)

    theirs = lax.dynamic_index_in_dim(part, 1 - core, 0, keepdims=False)
    mine = lax.dynamic_index_in_dim(part, core, 0, keepdims=False)
    total = add(mine, swap(theirs, "band", bands, 1))
    steps = [("member", count, 1 << i) for i in range(count.bit_length() - 1)]
    steps += [("band", bands, 1 << i) for i in range(1, bands.bit_length() - 1)]
    aside = None
    for i, (axis, size, bit) in enumerate(steps):
        got = swap(total, axis, size, bit)
        if i == 0:
            aside = beside(total)
            got, aside = lax.optimization_barrier((got, aside))
        total = add(total, got)
    other = swap(total, "band", bands, 1)
    low = jnp.where(core == 0, total, other)
    high = jnp.where(core == 0, other, total)
    return jnp.stack([low, high]).astype(F32), aside


def local(mesh_shape, fields, w_qkv, w_out, decoder_weight, window_reach, truth, radii):
    members, own, width = fields.shape
    heads = window_reach.shape[0]
    head = width // heads
    channels = decoder_weight.shape[0]
    scales = radii.shape[0]
    bands, member_count = mesh_shape["band"], mesh_shape["member"]
    members_total = members * member_count
    scale = head**-0.5
    band = lax.axis_index("band")
    core = band % 2
    info = jnp.concatenate(
        [
            jnp.stack([core, band == 0, band == bands - 1, 0]).astype(jnp.int32),
            window_reach.astype(jnp.int32),
        ]
    )
    inside = swap_pairs(bands, 0)
    across = swap_pairs(bands, 1) + [(0, 0), (bands - 1, bands - 1)]

    def exchange(block, dim, size):
        last = block.shape[dim] - size
        near = lax.dynamic_slice_in_dim(block, (1 - core) * last, size, dim)
        far = lax.dynamic_slice_in_dim(block, core * last, size, dim)
        return lax.ppermute(near, "band", inside), lax.ppermute(far, "band", across)

    x_near, x_far = exchange(fields, 1, HALO)
    truth_t = jnp.pad(truth.T, ((0, 0), (0, LANES - channels)))
    t_near, t_far = exchange(truth_t, 0, MARGIN)
    dec = jnp.pad(decoder_weight, ((0, LANES - channels), (0, 0)))

    cols = 2 * LANES
    steps = width // cols
    pairs = cols // LANES
    whole = lambda shape: pl.BlockSpec(shape, lambda i, s: (0,) * len(shape))
    inner = own - 2 * WIN
    main_rows = inner + EDGE
    col_block = lambda rows: pl.BlockSpec((members, rows, cols), lambda i, s: (0, 0, i))
    params = pltpu.CompilerParams(
        dimension_semantics=("arbitrary",), vmem_limit_bytes=48 * 1024 * 1024
    )
    group_block = lambda rows: pl.BlockSpec((members, rows, cols), lambda i, s: (0, 0, jnp.minimum(i, steps - 1)))
    group_weight = lambda third: pl.BlockSpec(
        (width, cols), lambda i, s: (0, third * steps + jnp.minimum(i, steps - 1))
    )
    work_set = [
        pltpu.VMEM((members, pairs, 2, own + 2 * HALO, LANES), BF16),
        pltpu.VMEM((members, pairs, 2, own + 2 * HALO, 2 * LANES), BF16),
        pltpu.VMEM((members, own + 2 * HALO, cols), BF16),
    ]
    q_own, k_own, v_own, hid_a, fc_a = pl.pallas_call(
        functools.partial(main_kernel, scale),
        grid_spec=pltpu.PrefetchScalarGridSpec(
            num_scalar_prefetch=1,
            grid=(steps + 1,),
            in_specs=[
                whole((members, own, width)),
                whole((members, HALO, width)),
                group_weight(0),
                group_weight(1),
                group_weight(2),
                pl.BlockSpec(memory_space=pl.ANY),
                whole((LANES, width)),
            ],
            out_specs=[
                group_block(own),
                group_block(own),
                group_block(own),
                whole((members, main_rows, width)),
                whole((members, main_rows, LANES)),
            ],
            scratch_shapes=work_set * 2
            + [
                pltpu.VMEM((members, main_rows, width), BF16),
                pltpu.VMEM((EDGE, width), BF16),
                pltpu.VMEM((2, WIN, KEYS), jnp.int32),
                pltpu.VMEM((width, width), BF16),
                pltpu.SemaphoreType.DMA,
            ],
        ),
        out_shape=[jax.ShapeDtypeStruct((members, own, width), BF16)] * 3
        + [
            jax.ShapeDtypeStruct((members, main_rows, width), BF16),
            jax.ShapeDtypeStruct((members, main_rows, LANES), F32),
        ],
        compiler_params=params,
        cost_estimate=pl.CostEstimate(
            flops=2 * members * own * width * 5 * width, bytes_accessed=24 << 20, transcendentals=1 << 22
        ),
    )(info, fields, x_near, w_qkv, w_qkv, w_qkv, w_out, dec)

    member_pairs = [(i, i ^ 1) for i in range(member_count)]
    other_a = lax.ppermute(fc_a, "member", member_pairs)

    far_block = lambda rows, last: pl.BlockSpec(
        (members, rows, cols), lambda i, s: (0, s[0] * last, jnp.minimum(i, steps - 1))
    )
    hid_b, fc_b = pl.pallas_call(
        functools.partial(edge_kernel, scale),
        grid_spec=pltpu.PrefetchScalarGridSpec(
            num_scalar_prefetch=1,
            grid=(steps + 1,),
            in_specs=[
                pl.BlockSpec((members, WIN, width), lambda i, s: (0, s[0] * (own // WIN - 1), 0)),
                whole((members, HALO, width)),
                group_weight(0),
                group_weight(1),
                group_weight(2),
                far_block(WIN, own // WIN - 1),
                far_block(2 * WIN, own // (2 * WIN) - 1),
                far_block(2 * WIN, own // (2 * WIN) - 1),
                pl.BlockSpec(memory_space=pl.ANY),
                whole((LANES, width)),
            ],
            out_specs=[whole((members, EDGE, width)), whole((members, EDGE, LANES))],
            scratch_shapes=[
                pltpu.VMEM((members, pairs, 2, FRAME, LANES), BF16),
                pltpu.VMEM((members, pairs, 2, FRAME, 2 * LANES), BF16),
                pltpu.VMEM((members, EDGE, cols), BF16),
            ]
            * 2
            + [
                pltpu.VMEM((members, EDGE, width), BF16),
                pltpu.VMEM((members, EDGE, width), BF16),
                pltpu.VMEM((2, WIN, KEYS), jnp.int32),
                pltpu.VMEM((width, width), BF16),
                pltpu.SemaphoreType.DMA,
            ],
        ),
        out_shape=[
            jax.ShapeDtypeStruct((members, EDGE, width), BF16),
            jax.ShapeDtypeStruct((members, EDGE, LANES), F32),
        ],
        compiler_params=params,
        cost_estimate=pl.CostEstimate(
            flops=2 * members * own * width * 2 * width, bytes_accessed=14 << 20, transcendentals=1 << 21
        ),
    )(info, fields, x_far, w_qkv, w_qkv, w_qkv, q_own, k_own, v_own, w_out, dec)
    other_b = lax.ppermute(fc_b, "member", member_pairs)

    chunks = width // LANES // 2
    keep_rows = chunks * channels + 16
    tiles = -(-(own + 2 * RMAX) // SCORE_ROWS)
    f_rows = (tiles - 1) * SCORE_ROWS + 2 * LANES
    s_rows = own + LANES
    smem = pl.BlockSpec(memory_space=pltpu.SMEM)
    vmem = pl.BlockSpec(memory_space=pltpu.VMEM)
    cot, part = pl.pallas_call(
        functools.partial(score_kernel, channels, members_total),
        in_specs=[smem, smem] + [vmem] * 9,
        out_specs=[vmem, vmem],
        out_shape=[
            jax.ShapeDtypeStruct((own, members * LANES), BF16),
            jax.ShapeDtypeStruct((2, keep_rows, LANES), BF16),
        ],
        scratch_shapes=[
            pltpu.VMEM((f_rows, (2 * members + 1) * LANES), BF16),
            pltpu.VMEM((f_rows, (2 * members + 1) * LANES), BF16),
            pltpu.VMEM((scales, s_rows, members * LANES), BF16),
            pltpu.VMEM((scales, s_rows, members * LANES), BF16),
        ],
        compiler_params=pltpu.CompilerParams(vmem_limit_bytes=48 * 1024 * 1024),
    )(info, radii, fc_a, fc_b, other_a, other_b, truth_t, t_near, t_far, hid_a, hid_b)

    def pull_back(sent):
        cot_now, _ = lax.optimization_barrier((cot, sent))
        return pl.pallas_call(
            grad_kernel,
            grid=(members, 2),
            in_specs=[
                pl.BlockSpec((own // 2, LANES), lambda m, h: (h, m)),
                pl.BlockSpec((LANES, width), lambda m, h: (0, 0)),
            ],
            out_specs=pl.BlockSpec((1, own // 2, width), lambda m, h: (m, h, 0)),
            out_shape=jax.ShapeDtypeStruct((members, own, width), BF16),
            cost_estimate=pl.CostEstimate(
                flops=2 * members * own * LANES * width, bytes_accessed=8 << 20, transcendentals=0
            ),
        )(cot_now, dec)

    summed, hidden_grad = reduce_all(part, mesh_shape, pull_back)
    decoder_grad = summed[:, : chunks * channels].reshape(2 * chunks, channels, LANES)
    decoder_grad = decoder_grad.transpose(1, 0, 2).reshape(channels, width)
    decoder_grad = decoder_grad / math.sqrt(members_total * own * bands)
    score = summed[0, chunks * channels, 0] + summed[0, chunks * channels + 1, 0]
    mean_score = score / (scales * channels * own * bands)
    return (mean_score, decoder_grad, hidden_grad)


def solution(mesh):
    placed = (P("member", "band", None), P(), P(), P(), P(), P(None, "band"), P())
    return jax.shard_map(
        functools.partial(local, dict(mesh.shape)),
        mesh=mesh,
        in_specs=placed,
        out_specs=(P(), P(), P("member", "band", None)),
        check_vma=False,
    )
```

```python
import functools
import math

import jax
import jax.numpy as jnp
from jax import lax
from jax.experimental import pallas as pl
from jax.experimental.pallas import tpu as pltpu
from jax.sharding import PartitionSpec as P

WIN = 128
RMAX = 16
MARGIN = 2 * RMAX
HALO = WIN + MARGIN
LANES = 128
KEYS = 3 * LANES
EDGE = HALO
FRAME = EDGE + 2 * WIN
WIDE = -(-FRAME // LANES) * LANES
SCORE_ROWS = 144
CHUNK = 512
SOFT = 0.1 * 0.1
F32 = jnp.float32
BF16 = jnp.bfloat16
NEG = -1e30
NT = (((1,), (1,)), ((), ()))
TN = (((0,), (0,)), ((), ()))


def mm(a, b):
    return jnp.dot(a, b, preferred_element_type=F32)


def half_masks():
    lane = lax.broadcasted_iota(jnp.int32, (1, LANES), 1)
    low = jnp.where(lane < LANES // 2, 1.0, 0.0).astype(BF16)
    return low, (1.0 - low.astype(F32)).astype(BF16)


def put_keys(kz, m, p, rows, piece):
    for h, mask in enumerate(half_masks()):
        kz[m, p, h, rows, :] = piece * mask


def put_values(vz, m, p, rows, piece):
    for h, mask in enumerate(half_masks()):
        vz[m, p, h, rows, :LANES] = piece * mask


def put_ones(vz, pairs):
    shape = vz.shape[:2] + vz.shape[3:4] + (LANES,)
    for h, mask in enumerate(half_masks()):
        vz[:, :, h, :, LANES:] = jnp.broadcast_to(mask.reshape(1, 1, 1, LANES), shape)


def distances(rows, keys, offset):
    qpos = lax.broadcasted_iota(jnp.int32, (rows, keys), 0) + offset
    return jnp.abs(qpos - lax.broadcasted_iota(jnp.int32, (rows, keys), 1))


def take(ref, *at):
    return ref[at]


def keep(ref, m, rows, lanes, values):
    ref[m, rows, lanes] = values


def attend_all(blocks, kz, vz, beside=()):
    def score(block):
        q, m, p, start = block[:4]
        window = pl.ds(start, block[7])
        keys = jnp.concatenate([kz[m, p, 0, window, :], kz[m, p, 1, window, :]], axis=0)
        return lax.dot_general(q(), keys, NT, preferred_element_type=F32)

    def soften(logits, block):
        away, reach, count = block[4](), block[5], block[7]
        parts = []
        for h in range(2):
            one = jnp.where(away <= reach[h], logits[:, h * count : (h + 1) * count], NEG)
            peak = jnp.max(one, axis=1, keepdims=True)
            parts.append(jnp.exp(one - peak).astype(BF16))
        return jnp.concatenate(parts, axis=1)

    def finish(probs, block):
        m, p, start = block[1:4]
        window = pl.ds(start, block[7])
        values = jnp.concatenate([vz[m, p, 0, window, :], vz[m, p, 1, window, :]], axis=0)
        mixed = mm(probs, values)
        block[6]((mixed[:, :LANES] / mixed[:, LANES:]).astype(BF16))

    beside = list(beside)
    total = len(beside)
    logits = score(blocks[0])
    probs = None
    for i, block in enumerate(blocks):
        following = score(blocks[i + 1]) if i + 1 < len(blocks) else None
        while beside and len(beside) * len(blocks) > (len(blocks) - 1 - i) * total:
            beside.pop(0)()
        if probs is not None:
            finish(probs, blocks[i - 1])
        probs = soften(logits, block)
        logits = following
    finish(probs, blocks[-1])


def main_kernel(
    scale, info, x, xh, wq, wk, wv, wo_hbm, dec, truth, q_out, k_out, v_out, hid, fc, truth_t, t_near, t_far,
    kz0, vz0, qs0, kz1, vz1, qs1, att, res, far, far_edge, wo, sem, wide,
):
    step = pl.program_id(0)
    members, own, width = x.shape
    cols = wq.shape[1]
    pairs = cols // LANES
    groups = width // cols
    sets = ((kz0, vz0, qs0), (kz1, vz1, qs1))
    lower = info[0] == 1
    halo_at = jnp.where(lower, 0, HALO + own)
    near = jnp.where(lower, WIN, 0)
    edge = jnp.where(lower, 0, own - WIN + MARGIN)
    window_at = jnp.minimum(edge, own + 2 * HALO - WIDE)
    halo_rows = pl.ds(pl.multiple_of(halo_at, 32), HALO)
    near_from = pl.ds(pl.multiple_of(near, 32), MARGIN)
    near_at = pl.ds(pl.multiple_of(halo_at + near, 32), MARGIN)
    inner = own - 2 * WIN
    weight_copy = pltpu.make_async_copy(wo_hbm, wo, sem)

    def own_chunk(kind, m, first, rows, kz, vz, qs):
        weight = (wq, wk, wv)[kind]
        at, to = pl.ds(first, rows), pl.ds(HALO + first, rows)
        made = mm(x[m, at, :], weight[...]).astype(BF16)
        if kind == 0:
            made = (made.astype(F32) * scale).astype(BF16)
            qs[m, to, :] = made
        else:
            for p in range(pairs):
                put = (put_keys, put_values)[kind - 1]
                put((kz, vz)[kind - 1], m, p, to, made[:, p * LANES : (p + 1) * LANES])
        (q_out, k_out, v_out)[kind][m, at, :] = made

    def halo_chunk(kind, kz, vz):
        made = mm(xh[...].reshape(members * HALO, width), (wk, wv)[kind][...]).astype(BF16)
        for m in range(members):
            for p in range(pairs):
                put = (put_keys, put_values)[kind]
                put((kz, vz)[kind], m, p, halo_rows, made[m * HALO : (m + 1) * HALO, p * LANES : (p + 1) * LANES])

    def near_chunk(qs):
        rows = jnp.concatenate([xh[m, near_from, :] for m in range(members)], axis=0)
        made = (mm(rows, wq[...]).astype(BF16).astype(F32) * scale).astype(BF16)
        for m in range(members):
            qs[m, near_at, :] = made[m * MARGIN : (m + 1) * MARGIN]

    def projections(kz, vz, qs):
        todo = []
        for kind in (1, 2, 0):
            for m in range(members):
                for first in range(0, own, CHUNK):
                    todo.append(functools.partial(own_chunk, kind, m, first, CHUNK, kz, vz, qs))
            todo.append(functools.partial(halo_chunk, kind - 1, kz, vz) if kind else functools.partial(near_chunk, qs))
        return todo

    def attention(group, kz, vz, qs, beside=()):
        blocks = []
        for p in range(pairs):
            reach = [info[4 + (group * pairs + p) * 2 + h] for h in range(2)]
            lanes = slice(p * LANES, (p + 1) * LANES)
            out_lanes = pl.ds(pl.multiple_of(group * cols + p * LANES, LANES), LANES)
            for m in range(members):
                for b in range(inner // WIN):
                    first = HALO + WIN + b * WIN
                    blocks.append(
                        (
                            functools.partial(take, qs, m, pl.ds(first, WIN), lanes),
                            m,
                            p,
                            first - WIN,
                            functools.partial(take, far, slice(None), slice(None)),
                            reach,
                            functools.partial(keep, att, m, pl.ds(b * WIN, WIN), out_lanes),
                            KEYS,
                        )
                    )
                blocks.append(
                    (
                        functools.partial(take, qs, m, pl.ds(pl.multiple_of(edge + WIN, 32), EDGE), lanes),
                        m,
                        p,
                        pl.multiple_of(window_at, 32),
                        functools.partial(take, far_edge, slice(None), slice(None)),
                        reach,
                        functools.partial(keep, att, m, pl.ds(inner, EDGE), out_lanes),
                        WIDE,
                    )
                )
        attend_all(blocks, kz, vz, beside)

    @pl.when(step == 0)
    def _():
        weight_copy.start()
        channels = truth.shape[0]
        wide[:channels, :] = truth[...]
        wide[channels:, :] = jnp.zeros((LANES - channels, own), F32)
        for tile in range(own // LANES):
            tokens = slice(tile * LANES, (tile + 1) * LANES)
            truth_t[tokens, :] = wide[:, tokens].T
        t_near[...] = truth_t[pl.ds(pl.multiple_of(jnp.where(lower, 0, own - MARGIN), 32), MARGIN), :]
        t_far[...] = truth_t[pl.ds(pl.multiple_of(jnp.where(lower, own - MARGIN, 0), 32), MARGIN), :]
        for _, vz, _ in sets:
            put_ones(vz, pairs)
        far[...] = distances(WIN, KEYS, WIN)
        far_edge[...] = distances(EDGE, WIDE, edge + WIN - window_at)
        for work in projections(*sets[0]):
            work()

    for parity in range(2):

        @pl.when((step > 0) & (step < groups) & (step % 2 == parity))
        def _():
            attention(step - 1, *sets[1 - parity], beside=projections(*sets[parity]))

    @pl.when(step == groups)
    def _():
        attention(step - 1, *sets[(groups - 1) % 2])
        weight_copy.wait()
        own_first = jnp.where(lower, MARGIN, 0)
        from_own = pl.ds(pl.multiple_of(jnp.where(lower, 0, own - WIN), 32), WIN)
        for m in range(members):
            res[pl.ds(pl.multiple_of(own_first, 32), WIN), :] = x[m, from_own, :]
            res[pl.ds(pl.multiple_of(jnp.where(lower, 0, WIN), 32), MARGIN), :] = xh[m, near_from, :]
            mixed = mm(att[m], wo[...])
            hid[m, :inner, :] = (mixed[:inner] + x[m, WIN : own - WIN, :].astype(F32)).astype(BF16)
            hid[m, inner:, :] = (mixed[inner:] + res[...].astype(F32)).astype(BF16)
            fc[m] = lax.dot_general(hid[m], dec[...], NT, preferred_element_type=F32)


def edge_kernel(
    scale, info, x, xh, wq, wk, wv, qi, ki, vi, wo_hbm, dec, hid, fc, kz0, vz0, qs0, kz1, vz1, qs1, att, res, far, wo, sem
):
    step = pl.program_id(0)
    members, _, width = x.shape
    cols = wq.shape[1]
    pairs = cols // LANES
    groups = width // cols
    sets = ((kz0, vz0, qs0), (kz1, vz1, qs1))
    lower = info[0] == 0
    own_rows = pl.ds(pl.multiple_of(jnp.where(lower, HALO, 0), 32), 2 * WIN)
    halo_rows = pl.ds(pl.multiple_of(jnp.where(lower, 0, 2 * WIN), 32), HALO)
    near_from = pl.ds(pl.multiple_of(jnp.where(lower, WIN, 0), 32), MARGIN)
    own_at = pl.ds(pl.multiple_of(jnp.where(lower, MARGIN, 0), 32), WIN)
    near_at = pl.ds(pl.multiple_of(jnp.where(lower, 0, WIN), 32), MARGIN)
    low = jnp.where(info[1] == 1, HALO, 0)
    high = jnp.where(info[2] == 1, 2 * WIN, FRAME)
    weight_copy = pltpu.make_async_copy(wo_hbm, wo, sem)

    def own_chunk(kind, m, p, target):
        lanes = slice(p * LANES, (p + 1) * LANES)
        (put_keys, put_values)[kind](target, m, p, own_rows, (ki, vi)[kind][m, :, lanes])

    def halo_chunk(kind, m, kz, vz):
        made = mm(xh[m], (wk, wv)[kind][...]).astype(BF16)
        for p in range(pairs):
            (put_keys, put_values)[kind]((kz, vz)[kind], m, p, halo_rows, made[:, p * LANES : (p + 1) * LANES])

    def query_chunk(qs):
        rows = jnp.concatenate([xh[m, near_from, :] for m in range(members)], axis=0)
        made = (mm(rows, wq[...]).astype(BF16).astype(F32) * scale).astype(BF16)
        for m in range(members):
            qs[m, own_at, :] = qi[m]
            qs[m, near_at, :] = made[m * MARGIN : (m + 1) * MARGIN]

    def projections(kz, vz, qs):
        todo = []
        for kind in range(2):
            for m in range(members):
                todo.append(functools.partial(halo_chunk, kind, m, kz, vz))
                for p in range(pairs):
                    todo.append(functools.partial(own_chunk, kind, m, p, (kz, vz)[kind]))
        todo.append(functools.partial(query_chunk, qs))
        return todo

    def attention(group, kz, vz, qs, beside=()):
        blocks = []
        for p in range(pairs):
            reach = [info[4 + (group * pairs + p) * 2 + h] for h in range(2)]
            lanes = slice(p * LANES, (p + 1) * LANES)
            out_lanes = pl.ds(pl.multiple_of(group * cols + p * LANES, LANES), LANES)
            for m in range(members):
                blocks.append(
                    (
                        functools.partial(take, qs, m, slice(None), lanes),
                        m,
                        p,
                        0,
                        functools.partial(take, far, slice(None), slice(None)),
                        reach,
                        functools.partial(keep, att, m, slice(None), out_lanes),
                        WIDE,
                    )
                )
        attend_all(blocks, kz, vz, beside)

    @pl.when(step == 0)
    def _():
        weight_copy.start()
        for _, vz, _ in sets:
            put_ones(vz, pairs)
        for kz, vz, _ in sets:
            kz[:, :, :, FRAME:, :] = jnp.zeros((members, pairs, 2, WIDE - FRAME, LANES), BF16)
            vz[:, :, :, FRAME:, :LANES] = jnp.zeros((members, pairs, 2, WIDE - FRAME, LANES), BF16)
        kpos = lax.broadcasted_iota(jnp.int32, (EDGE, WIDE), 1)
        far[...] = jnp.where((kpos >= low) & (kpos < high), distances(EDGE, WIDE, WIN), 1 << 20)
        for work in projections(*sets[0]):
            work()

    for parity in range(2):

        @pl.when((step > 0) & (step < groups) & (step % 2 == parity))
        def _():
            attention(step - 1, *sets[1 - parity], beside=projections(*sets[parity]))

    @pl.when(step == groups)
    def _():
        attention(step - 1, *sets[(groups - 1) % 2])
        weight_copy.wait()
        for m in range(members):
            res[m, own_at, :] = x[m]
            res[m, near_at, :] = xh[m, near_from, :]
        mixed = mm(att[...].reshape(members * EDGE, width), wo[...])
        hidden = (mixed + res[...].reshape(members * EDGE, width).astype(F32)).astype(BF16)
        hid[...] = hidden.reshape(members, EDGE, width)
        fc[...] = lax.dot_general(hidden, dec[...], NT, preferred_element_type=F32).reshape(
            members, EDGE, dec.shape[0]
        )


def toeplitz(radii, scale_index, rows, cols):
    reach = radii[scale_index].astype(F32)
    spread = 0.5 * reach
    twice = 2.0 * spread * spread

    def weigh(shape, shift):
        away = lax.broadcasted_iota(jnp.int32, shape, 1) - shift
        far = jnp.abs(away).astype(F32)
        return jnp.where(far <= reach, jnp.exp(-(far * far) / twice), 0.0)

    line = weigh((8, LANES), RMAX)
    total = jnp.sum(line, axis=1, keepdims=True)[:1]
    shift = lax.broadcasted_iota(jnp.int32, (rows, cols), 0) + RMAX
    return weigh((rows, cols), shift) / total


def split(values):
    high = values.astype(BF16)
    return high, (values - high.astype(F32)).astype(BF16)


def score_kernel(
    channels, members_total, info, radii, fa, fb, ga, gb, truth, t_near, t_far, hid_a, hid_b, cot, mine, theirs, fh, fl, sh, sl
):
    members, _, _ = fa.shape
    own = truth.shape[0]
    scales = radii.shape[0]
    inner = own - 2 * WIN
    rows = SCORE_ROWS
    window = 2 * LANES
    lower = info[0] == 0
    begins, ends = info[1] == 1, info[2] == 1
    far_at = pl.ds(pl.multiple_of(jnp.where(lower, 0, inner + EDGE), 32), EDGE)
    near_at = pl.ds(pl.multiple_of(jnp.where(lower, inner + EDGE, 0), 32), EDGE)
    total_rows = own + 2 * MARGIN

    def put(at, column, values):
        lanes = slice(column * LANES, (column + 1) * LANES)
        fh[at, lanes], fl[at, lanes] = split(values)

    for side, (f_main, f_far) in enumerate(((fa, fb), (ga, gb))):
        for m in range(members):
            column = side * members + m
            put(pl.ds(EDGE, inner), column, f_main[m, :inner, :])
            put(near_at, column, f_main[m, inner:, :])
            put(far_at, column, f_far[m])
    put(pl.ds(MARGIN, own), 2 * members, truth[...])
    put(pl.ds(pl.multiple_of(jnp.where(lower, 0, MARGIN + own), 32), MARGIN), 2 * members, t_far[...])
    put(pl.ds(pl.multiple_of(jnp.where(lower, MARGIN + own, 0), 32), MARGIN), 2 * members, t_near[...])
    for ref in (fh, fl):
        ref[total_rows:, :] = jnp.zeros((ref.shape[0] - total_rows, ref.shape[1]), BF16)

        @pl.when(begins)
        def _():
            ref[:MARGIN, :] = jnp.zeros((MARGIN, ref.shape[1]), BF16)

        @pl.when(ends)
        def _():
            ref[MARGIN + own : total_rows, :] = jnp.zeros((MARGIN, ref.shape[1]), BF16)

    tiles = -(-(own + 2 * RMAX) // rows)
    for ref in (sh, sl):
        spare = ref.shape[1] - tiles * rows
        ref[:, tiles * rows :, :] = jnp.zeros((scales, spare, ref.shape[2]), BF16)

    weights = [split(toeplitz(radii, s, rows, window)) for s in range(scales)]
    forward = jnp.concatenate([jnp.concatenate([h, h, l], axis=1) for h, l in weights], axis=0)
    backward = jnp.concatenate(
        [h[:LANES] for h, l in weights] + [h[:LANES] for h, l in weights] + [l[:LANES] for h, l in weights],
        axis=1,
    )
    first_valid = jnp.where(begins, RMAX, 0)
    last_valid = jnp.where(ends, RMAX + own, 2 * RMAX + own)
    pair_weight = 1.0 / (members_total * (members_total - 1))
    others = 2 * members
    total = jnp.zeros((rows, LANES), F32)
    for tile in range(tiles):
        at = pl.ds(tile * rows, window)
        stacked = jnp.concatenate([fh[at, :], fl[at, :], fh[at, :]], axis=0)
        smooth = mm(forward, stacked)
        line = lax.broadcasted_iota(jnp.int32, (rows, LANES), 0) + tile * rows
        valid = jnp.where((line >= first_valid) & (line < last_valid), 1.0, 0.0)
        tile_score = jnp.zeros((rows, LANES), F32)
        for s in range(scales):
            values = [
                smooth[s * rows : (s + 1) * rows, i * LANES : (i + 1) * LANES] for i in range(others + 1)
            ]

            def gap(a, b):
                away = values[a] - values[b]
                square = away * away + SOFT
                inverse = lax.rsqrt(square)
                return away * inverse, square * inverse

            skill = jnp.zeros((rows, LANES), F32)
            spread = jnp.zeros((rows, LANES), F32)
            slopes = []
            cross = [jnp.zeros((rows, LANES), F32) for _ in range(members)]
            for m in range(members):
                slope, size = gap(m, others)
                skill = skill + size
                slopes.append(slope)
            for a in range(members):
                for b in range(a + 1, others):
                    slope, size = gap(a, b)
                    cross[a] = cross[a] + slope
                    if b < members:
                        cross[b] = cross[b] - slope
                        spread = spread + size
                    else:
                        spread = spread + 0.5 * size
            tile_score = tile_score + (skill * (1.0 / members_total) - pair_weight * spread)
            for m in range(members):
                slope = (slopes[m] * (1.0 / members_total) - pair_weight * cross[m]) * valid
                keep, lanes = pl.ds(tile * rows, rows), slice(m * LANES, (m + 1) * LANES)
                sh[s, keep, lanes], sl[s, keep, lanes] = split(slope)
        scored = (line >= RMAX) & (line < RMAX + own)
        total = total + jnp.where(scored, tile_score, 0.0)
    lane = lax.broadcasted_iota(jnp.int32, (rows, LANES), 1)
    total = jnp.where(lane < channels, total, 0.0)
    score = jnp.sum(jnp.sum(total, axis=0, keepdims=True), axis=1, keepdims=True)

    for tile in range(own // LANES):
        at = pl.ds(tile * LANES, window)
        high = [sh[s, at, :] for s in range(scales)]
        low = [sl[s, at, :] for s in range(scales)]
        stacked = jnp.concatenate(high + low + high, axis=0)
        cot[tile * LANES : (tile + 1) * LANES, :] = mm(backward, stacked).astype(BF16)

    near_own = pl.ds(pl.multiple_of(jnp.where(lower, own - WIN, 0), 32), WIN)
    far_own = pl.ds(pl.multiple_of(jnp.where(lower, 0, own - WIN), 32), WIN)
    near_skip = pl.multiple_of(jnp.where(lower, 0, MARGIN), 32)
    far_skip = pl.multiple_of(jnp.where(lower, MARGIN, 0), 32)
    width = hid_a.shape[2]
    grad = jnp.zeros((LANES, width), F32)
    for m in range(members):
        lanes = slice(m * LANES, (m + 1) * LANES)
        for c_rows, ref, h_rows in (
            (pl.ds(WIN, inner), hid_a, pl.ds(0, inner)),
            (near_own, hid_a, pl.ds(inner + near_skip, WIN)),
            (far_own, hid_b, pl.ds(far_skip, WIN)),
        ):
            grad = grad + lax.dot_general(cot[c_rows, lanes], ref[m, h_rows, :], TN, preferred_element_type=F32)
    chunks = width // LANES // 2
    extra = mine.shape[0] - chunks * channels
    line = lax.broadcasted_iota(jnp.int32, (extra, LANES), 0)
    score_high = score.astype(BF16).astype(F32)
    tail = jnp.where(line == 0, score_high, jnp.where(line == 1, score - score_high, 0.0)).astype(BF16)
    for c in range(chunks):
        low_part = grad[:channels, c * LANES : (c + 1) * LANES].astype(BF16)
        high_part = grad[:channels, (chunks + c) * LANES : (chunks + c + 1) * LANES].astype(BF16)
        rows_at = slice(c * channels, (c + 1) * channels)
        mine[rows_at, :] = jnp.where(lower, low_part, high_part)
        theirs[rows_at, :] = jnp.where(lower, high_part, low_part)
    mine[chunks * channels :, :] = tail
    theirs[chunks * channels :, :] = tail


def assemble_kernel(scale_grad, scale_score, total, other, grad, score):
    channels = grad.shape[0]
    chunks = grad.shape[1] // LANES // 2
    even = lax.axis_index("band") % 2 == 0
    for c in range(chunks):
        rows = slice(c * channels, (c + 1) * channels)
        ours, others = total[rows, :].astype(F32) * scale_grad, other[rows, :].astype(F32) * scale_grad
        grad[:, c * LANES : (c + 1) * LANES] = jnp.where(even, ours, others)
        grad[:, (chunks + c) * LANES : (chunks + c + 1) * LANES] = jnp.where(even, others, ours)
    terms = total[chunks * channels :, :].astype(F32)
    score[0, 0] = (terms[0, 0] + terms[1, 0]) * scale_score


def grad_kernel(cot, dec, out):
    out[0] = mm(cot[...], dec[...]).astype(BF16)


def swap_pairs(count, first):
    pairs = []
    for i in range(first, count - 1, 2):
        pairs += [(i, i + 1), (i + 1, i)]
    return pairs


def reduce_all(mine, theirs, mesh_shape, beside):
    bands, count = mesh_shape["band"], mesh_shape["member"]

    def swap(values, axis, size, bit):
        return lax.ppermute(values, axis, [(i, i ^ bit) for i in range(size)])

    def add(mine, theirs):
        return (mine.astype(F32) + theirs.astype(F32)).astype(BF16)

    total = add(mine, swap(theirs, "band", bands, 1))
    steps = [("member", count, 1 << i) for i in range(count.bit_length() - 1)]
    steps += [("band", bands, 1 << i) for i in range(1, bands.bit_length() - 1)]
    aside = None
    for i, (axis, size, bit) in enumerate(steps):
        got = swap(total, axis, size, bit)
        if i == len(steps) - 1:
            aside = beside(total)
            got, aside = lax.optimization_barrier((got, aside))
        total = add(total, got)
    other = swap(total, "band", bands, 1)
    return total, other, aside


def local(mesh_shape, fields, w_qkv, w_out, decoder_weight, window_reach, truth, radii):
    members, own, width = fields.shape
    heads = window_reach.shape[0]
    head = width // heads
    channels = decoder_weight.shape[0]
    scales = radii.shape[0]
    bands, member_count = mesh_shape["band"], mesh_shape["member"]
    members_total = members * member_count
    scale = head**-0.5
    band = lax.axis_index("band")
    core = band % 2
    info = jnp.concatenate(
        [
            jnp.stack([core, band == 0, band == bands - 1, 0]).astype(jnp.int32),
            window_reach.astype(jnp.int32),
        ]
    )
    inside = swap_pairs(bands, 0)
    across = swap_pairs(bands, 1) + [(0, 0), (bands - 1, bands - 1)]

    last = own - HALO
    x_near = lax.ppermute(lax.dynamic_slice_in_dim(fields, (1 - core) * last, HALO, 1), "band", inside)
    x_far = lax.ppermute(lax.dynamic_slice_in_dim(fields, core * last, HALO, 1), "band", across)
    dec = jnp.pad(decoder_weight, ((0, LANES - channels), (0, 0)))

    cols = 2 * LANES
    steps = width // cols
    pairs = cols // LANES
    whole = lambda shape: pl.BlockSpec(shape, lambda i, s: (0,) * len(shape))
    inner = own - 2 * WIN
    main_rows = inner + EDGE
    col_block = lambda rows: pl.BlockSpec((members, rows, cols), lambda i, s: (0, 0, i))
    params = pltpu.CompilerParams(
        dimension_semantics=("arbitrary",), vmem_limit_bytes=48 * 1024 * 1024
    )
    group_block = lambda rows: pl.BlockSpec((members, rows, cols), lambda i, s: (0, 0, jnp.minimum(i, steps - 1)))
    group_weight = lambda third: pl.BlockSpec(
        (width, cols), lambda i, s: (0, third * steps + jnp.minimum(i, steps - 1))
    )
    work_set = [
        pltpu.VMEM((members, pairs, 2, own + 2 * HALO, LANES), BF16),
        pltpu.VMEM((members, pairs, 2, own + 2 * HALO, 2 * LANES), BF16),
        pltpu.VMEM((members, own + 2 * HALO, cols), BF16),
    ]
    q_own, k_own, v_own, hid_a, fc_a, truth_t, t_near, t_far = pl.pallas_call(
        functools.partial(main_kernel, scale),
        grid_spec=pltpu.PrefetchScalarGridSpec(
            num_scalar_prefetch=1,
            grid=(steps + 1,),
            in_specs=[
                whole((members, own, width)),
                whole((members, HALO, width)),
                group_weight(0),
                group_weight(1),
                group_weight(2),
                pl.BlockSpec(memory_space=pl.ANY),
                whole((LANES, width)),
                whole((channels, own)),
            ],
            out_specs=[
                group_block(own),
                group_block(own),
                group_block(own),
                whole((members, main_rows, width)),
                whole((members, main_rows, LANES)),
                whole((own, LANES)),
                whole((MARGIN, LANES)),
                whole((MARGIN, LANES)),
            ],
            scratch_shapes=work_set * 2
            + [
                pltpu.VMEM((members, main_rows, width), BF16),
                pltpu.VMEM((EDGE, width), BF16),
                pltpu.VMEM((WIN, KEYS), jnp.int32),
                pltpu.VMEM((EDGE, WIDE), jnp.int32),
                pltpu.VMEM((width, width), BF16),
                pltpu.SemaphoreType.DMA,
                pltpu.VMEM((LANES, own), F32),
            ],
        ),
        out_shape=[jax.ShapeDtypeStruct((members, own, width), BF16)] * 3
        + [
            jax.ShapeDtypeStruct((members, main_rows, width), BF16),
            jax.ShapeDtypeStruct((members, main_rows, LANES), F32),
            jax.ShapeDtypeStruct((own, LANES), F32),
            jax.ShapeDtypeStruct((MARGIN, LANES), F32),
            jax.ShapeDtypeStruct((MARGIN, LANES), F32),
        ],
        compiler_params=params,
        cost_estimate=pl.CostEstimate(
            flops=2 * members * own * width * 5 * width, bytes_accessed=24 << 20, transcendentals=1 << 22
        ),
    )(info, fields, x_near, w_qkv, w_qkv, w_qkv, w_out, dec, truth)

    member_pairs = [(i, i ^ 1) for i in range(member_count)]
    other_a = lax.ppermute(fc_a, "member", member_pairs)

    far_block = lambda rows, last: pl.BlockSpec(
        (members, rows, cols), lambda i, s: (0, s[0] * last, jnp.minimum(i, steps - 1))
    )
    hid_b, fc_b = pl.pallas_call(
        functools.partial(edge_kernel, scale),
        grid_spec=pltpu.PrefetchScalarGridSpec(
            num_scalar_prefetch=1,
            grid=(steps + 1,),
            in_specs=[
                pl.BlockSpec((members, WIN, width), lambda i, s: (0, s[0] * (own // WIN - 1), 0)),
                whole((members, HALO, width)),
                group_weight(0),
                group_weight(1),
                group_weight(2),
                far_block(WIN, own // WIN - 1),
                far_block(2 * WIN, own // (2 * WIN) - 1),
                far_block(2 * WIN, own // (2 * WIN) - 1),
                pl.BlockSpec(memory_space=pl.ANY),
                whole((LANES, width)),
            ],
            out_specs=[whole((members, EDGE, width)), whole((members, EDGE, LANES))],
            scratch_shapes=[
                pltpu.VMEM((members, pairs, 2, WIDE, LANES), BF16),
                pltpu.VMEM((members, pairs, 2, WIDE, 2 * LANES), BF16),
                pltpu.VMEM((members, EDGE, cols), BF16),
            ]
            * 2
            + [
                pltpu.VMEM((members, EDGE, width), BF16),
                pltpu.VMEM((members, EDGE, width), BF16),
                pltpu.VMEM((EDGE, WIDE), jnp.int32),
                pltpu.VMEM((width, width), BF16),
                pltpu.SemaphoreType.DMA,
            ],
        ),
        out_shape=[
            jax.ShapeDtypeStruct((members, EDGE, width), BF16),
            jax.ShapeDtypeStruct((members, EDGE, LANES), F32),
        ],
        compiler_params=params,
        cost_estimate=pl.CostEstimate(
            flops=2 * members * own * width * 2 * width, bytes_accessed=14 << 20, transcendentals=1 << 21
        ),
    )(info, fields, x_far, w_qkv, w_qkv, w_qkv, q_own, k_own, v_own, w_out, dec)
    other_b = lax.ppermute(fc_b, "member", member_pairs)
    t_near = lax.ppermute(t_near, "band", inside)
    t_far = lax.ppermute(t_far, "band", across)

    chunks = width // LANES // 2
    keep_rows = chunks * channels + 16
    tiles = -(-(own + 2 * RMAX) // SCORE_ROWS)
    f_rows = (tiles - 1) * SCORE_ROWS + 2 * LANES
    s_rows = own + LANES
    smem = pl.BlockSpec(memory_space=pltpu.SMEM)
    vmem = pl.BlockSpec(memory_space=pltpu.VMEM)
    cot, mine, theirs = pl.pallas_call(
        functools.partial(score_kernel, channels, members_total),
        in_specs=[smem, smem] + [vmem] * 9,
        out_specs=[vmem, vmem, vmem],
        out_shape=[
            jax.ShapeDtypeStruct((own, members * LANES), BF16),
            jax.ShapeDtypeStruct((keep_rows, LANES), BF16),
            jax.ShapeDtypeStruct((keep_rows, LANES), BF16),
        ],
        scratch_shapes=[
            pltpu.VMEM((f_rows, (2 * members + 1) * LANES), BF16),
            pltpu.VMEM((f_rows, (2 * members + 1) * LANES), BF16),
            pltpu.VMEM((scales, s_rows, members * LANES), BF16),
            pltpu.VMEM((scales, s_rows, members * LANES), BF16),
        ],
        compiler_params=pltpu.CompilerParams(vmem_limit_bytes=48 * 1024 * 1024),
    )(info, radii, fc_a, fc_b, other_a, other_b, truth_t, t_near, t_far, hid_a, hid_b)

    def pull_back(sent):
        cot_now, _ = lax.optimization_barrier((cot, sent))
        return pl.pallas_call(
            grad_kernel,
            grid=(members, 2),
            compiler_params=pltpu.CompilerParams(vmem_limit_bytes=16 * 1024 * 1024),
            in_specs=[
                pl.BlockSpec((own // 2, LANES), lambda m, h: (h, m)),
                pl.BlockSpec((LANES, width), lambda m, h: (0, 0)),
            ],
            out_specs=pl.BlockSpec((1, own // 2, width), lambda m, h: (m, h, 0)),
            out_shape=jax.ShapeDtypeStruct((members, own, width), BF16),
            cost_estimate=pl.CostEstimate(
                flops=2 * members * own * LANES * width, bytes_accessed=8 << 20, transcendentals=0
            ),
        )(cot_now, dec)

    total, other, hidden_grad = reduce_all(mine, theirs, mesh_shape, pull_back)
    decoder_grad, mean_score = pl.pallas_call(
        functools.partial(
            assemble_kernel,
            1.0 / math.sqrt(members_total * own * bands),
            1.0 / (scales * channels * own * bands),
        ),
        in_specs=[vmem, vmem],
        out_specs=[vmem, smem],
        out_shape=[jax.ShapeDtypeStruct((channels, width), F32), jax.ShapeDtypeStruct((1, 1), F32)],
        compiler_params=pltpu.CompilerParams(vmem_limit_bytes=16 * 1024 * 1024),
    )(total, other)
    mean_score = mean_score.reshape(())
    return (mean_score, decoder_grad, hidden_grad)


def solution(mesh):
    placed = (P("member", "band", None), P(), P(), P(), P(), P(None, "band"), P())
    return jax.shard_map(
        functools.partial(local, dict(mesh.shape)),
        mesh=mesh,
        in_specs=placed,
        out_specs=(P(), P(), P("member", "band", None)),
        check_vma=False,
    )
```
